512 devices in a mesh: dp: 64 (over z, y), tensor: 8 (over x, core).
Axes of the slice: x: 4, y: 8, z: 8, core: 2. Of those that a mesh axis runs over, the one named last changes fastest.
Arguments:
- tool_len: int32 [512], P('dp'), may hold values from 1 to 32
- state_table: int32 [512, 32], replicated, may hold values from 0 to 511, as said below
- page_table: int32 [512, 8, 4], replicated, may hold values from 0 to 2047, as said below
- kda_pool: bfloat16 [32, 512, 128, 128], P('tensor', 'dp'), may hold values from -6 to 6
- latent_pool: bfloat16 [8, 2048, 32, 512], P('tensor', 'dp'), may hold values from -6 to 6
- kda_q: bfloat16 [512, 32, 4096], P('dp', None, 'tensor'), may hold values from -6 to 6
- kda_k: bfloat16 [512, 32, 4096], P('dp', None, 'tensor'), may hold values from -6 to 6
- kda_v: bfloat16 [512, 32, 4096], P('dp', None, 'tensor'), may hold values from -6 to 6
- kda_gate: bfloat16 [512, 32, 4096], P('dp', None, 'tensor'), may hold values from -1.2 to 0
- kda_beta: bfloat16 [512, 32, 32], P('dp', None, 'tensor'), may hold values from -6 to 6
- mla_q: bfloat16 [512, 32, 4096], P('dp', None, 'tensor'), may hold values from -384 to 384
- mla_new: bfloat16 [512, 32, 512], P('dp'), may hold values from -6 to 6
- w_uk: bfloat16 [32, 128, 512], P('tensor'), may hold values from -0.5 to 0.5
- w_uv: bfloat16 [32, 512, 128], P('tensor'), may hold values from -0.25 to 0.25
Outputs:
- gated_recall_output: bfloat16 [512, 32, 4096], P('dp', None, 'tensor')
- mla_out: bfloat16 [512, 32, 4096], P('dp', None, 'tensor')
The draws below stay inside these ranges and needn't reach their ends.
Inputs may be any that keep to these rules, and one draw needn't show every extreme that they name: `state_table`: for each head, every slot of its pool is named by exactly one row. For every index g of tensor, the records that the rows of one index of dp need in class g (their states of heads g * 4 to (g + 1) * 4 - 1 and their pages of class g) and that lie in the pools of one index of dp number at most 2, and exactly 2 for some pairs. `page_table`: for each class, every slot of its pool is named by exactly one page of one row; counted together with state_table as stated there.
All inputs are finite; a program needn't handle non-finite values.
Results may differ from the reference program's by a relative error of at most 0.015.
The reference program's roundings to bfloat16 on the way count: a program that leaves them out, or rounds other values in their place, can miss the bound.
Values may be sent and summed in bfloat16 or wider, within the bound.
A program may use at most 64 MiB of HBM per device.

```python
import math
import jax
import jax.numpy as jnp
from jax import lax

HEADS = 32
HD = 128
LAT = 512
ROWS_DEV = 8
CALLOUT_POSITIONS = 32
CTX = 1024
HPD = 4
PAGE = 32
CLASSES = 8
PC = 4
UNITS = 64
CAP = 2
ROWS = 512
SSLOTS = 512
PSLOTS = 2048
N_DP = 64


def build_tables(key):
    sequence_count = ROWS_DEV * N_DP
    state_table = jnp.zeros((sequence_count, HEADS), jnp.int32)
    page_table = jnp.zeros((sequence_count, CLASSES, PC), jnp.int32)
    worker_unit_index = jnp.arange(UNITS)
    dest_ids = jnp.arange(N_DP)[:, None]
    for group in range(CLASSES):
        lookup_matrix_lines = jax.random.split(jax.random.fold_in(key, 100 + group), 9)
        first = jax.random.randint(lookup_matrix_lines[0], (N_DP // 2,), 0, CAP + 1)
        first = first.at[0].set(CAP)
        counts = jnp.stack([first, CAP - first], axis=1).reshape(N_DP)
        counts = counts[jax.random.permutation(lookup_matrix_lines[1], N_DP)]
        bounds = jnp.cumsum(counts)
        offsets = jnp.sum((bounds[None, :] <= worker_unit_index[:, None]).astype(jnp.int32), axis=1)
        kinds = jnp.concatenate([jnp.repeat(jnp.arange(HPD), ROWS_DEV), jnp.full((ROWS_DEV * PC,), HPD)]).astype(jnp.int32)
        kinds = kinds[jax.random.permutation(lookup_matrix_lines[2], UNITS)]
        same_kind = kinds[:, None] == kinds[None, :]
        earlier = worker_unit_index[None, :] < worker_unit_index[:, None]
        ranks = jnp.sum((same_kind & earlier).astype(jnp.int32), axis=1)
        dest_perm = jax.random.permutation(lookup_matrix_lines[3], N_DP)
        owner_perm = jax.random.permutation(lookup_matrix_lines[4], N_DP)
        owner_inverse = jnp.argsort(owner_perm)
        owners = owner_inverse[(dest_perm[:, None] + offsets[None, :]) % N_DP]
        state_perm = jax.random.permutation(lookup_matrix_lines[5], jnp.broadcast_to(jnp.arange(ROWS_DEV), (N_DP, HPD, ROWS_DEV)), axis=2, independent=True)
        page_perm = jax.random.permutation(lookup_matrix_lines[6], jnp.broadcast_to(jnp.arange(ROWS_DEV * PC), (N_DP, ROWS_DEV * PC)), axis=1, independent=True)
        row_perm = jax.random.permutation(lookup_matrix_lines[7], jnp.broadcast_to(jnp.arange(ROWS_DEV), (N_DP, HPD, ROWS_DEV)), axis=2, independent=True)
        place_perm = jax.random.permutation(lookup_matrix_lines[8], jnp.broadcast_to(jnp.arange(ROWS_DEV * PC), (N_DP, ROWS_DEV * PC)), axis=1, independent=True)
        is_state = kinds < HPD
        head_local = jnp.minimum(kinds, HPD - 1)
        state_rank = jnp.minimum(ranks, ROWS_DEV - 1)
        state_slot = owners * ROWS_DEV + state_perm[owners, head_local[None, :], state_rank[None, :]]
        page_slot = owners * (ROWS_DEV * PC) + page_perm[owners, ranks[None, :]]
        state_row = dest_ids * ROWS_DEV + row_perm[dest_ids, head_local[None, :], state_rank[None, :]]
        placed = place_perm[dest_ids, ranks[None, :]]
        page_row = dest_ids * ROWS_DEV + placed // PC
        page_index = placed % PC
        head_col = jnp.broadcast_to(group * HPD + head_local[None, :], (N_DP, UNITS))
        state_table = state_table.at[jnp.where(is_state[None, :], state_row, sequence_count), head_col].set(state_slot.astype(jnp.int32), mode='drop')
        page_table = page_table.at[jnp.where(is_state[None, :], sequence_count, page_row), group, page_index].set(page_slot.astype(jnp.int32), mode='drop')
    return (state_table, page_table)


def draw_state_table(key, part):
    return build_tables(key)[0]


def draw_page_table(key, part):
    return build_tables(key)[1]


def draw_tool_len(key, part):
    key = jax.random.fold_in(key, 11)
    first, second, third = jax.random.split(key, 3)
    sequence_count = ROWS_DEV * N_DP
    lengths = jax.random.randint(first, (sequence_count,), 1, CALLOUT_POSITIONS + 1)
    longest = jax.random.randint(second, (), 0, sequence_count)
    shortest = (longest + 1 + jax.random.randint(third, (), 0, sequence_count - 1)) % sequence_count
    return lengths.at[longest].set(CALLOUT_POSITIONS).at[shortest].set(1).astype(jnp.int32)


def decay_rates(key, sequence_breadth, lowest, highest):
    return jnp.exp(jax.random.uniform(key, (sequence_breadth,), minval=math.log(lowest), maxval=math.log(highest)))


def draw_kda_gate(key, part):
    key = jax.random.fold_in(key, 7)
    lookup_matrix_lines = jax.random.split(key, 5)
    sequence_count = ROWS_DEV * N_DP
    sequence_breadth = HEADS * HD
    rates = decay_rates(lookup_matrix_lines[0], sequence_breadth, 0.003, 0.12)
    row_factor = jnp.exp(jax.random.uniform(lookup_matrix_lines[1], (sequence_count, 1, 1), minval=math.log(0.5), maxval=math.log(2.0)))
    jitter = jax.random.uniform(lookup_matrix_lines[2], (sequence_count, CALLOUT_POSITIONS, sequence_breadth), minval=0.5, maxval=1.5)
    emitted_spans = (jax.random.uniform(lookup_matrix_lines[3], (sequence_count, CALLOUT_POSITIONS, 1)) < 0.08).astype(jnp.float32)
    objective_amounts = emitted_spans * jax.random.uniform(lookup_matrix_lines[4], (sequence_count, CALLOUT_POSITIONS, sequence_breadth), minval=0.2, maxval=0.7)
    return (-(rates[None, None, :] * row_factor * jitter + objective_amounts)).astype(jnp.bfloat16)


def query_strengths(key, shape, lowest, highest):
    return jnp.exp(jax.random.uniform(key, shape, minval=math.log(lowest), maxval=math.log(highest)))


def draw_mla_q(key, part):
    key = jax.random.fold_in(key, 13)
    lookup_matrix_lines = jax.random.split(key, 4)
    sequence_count = ROWS_DEV * N_DP
    sequence_breadth = HEADS * HD
    base = jax.random.truncated_normal(lookup_matrix_lines[0], -6.0, 6.0, (sequence_count, CALLOUT_POSITIONS, sequence_breadth), jnp.float32)
    strengths = query_strengths(lookup_matrix_lines[1], (sequence_count, CALLOUT_POSITIONS, 1), 8.0, 32.0)
    token_ids = jnp.arange(CALLOUT_POSITIONS)[None, :, None]
    row_ids = jnp.arange(sequence_count)[:, None, None]
    chance = jnp.where(token_ids == 0, 0.3, 0.08)
    planted = jax.random.uniform(lookup_matrix_lines[2], (sequence_count, CALLOUT_POSITIONS, 1)) < chance
    forced_row = jax.random.randint(lookup_matrix_lines[3], (), 0, sequence_count)
    planted = planted | (row_ids == forced_row) & (token_ids == 0)
    factor = jnp.where(planted, strengths, 1.0)
    return (base * factor).astype(jnp.bfloat16)


def steps_of(rng, shape, cuts, least, top_value):
    gain, own = 1.0, jax.random.fold_in(rng, 6)
    for axis_at, blocks in cuts:
        heights = jnp.exp(jax.random.uniform(jax.random.fold_in(own, axis_at), (blocks,), jnp.float32, least / len(cuts), top_value / len(cuts)))
        gain = gain * jnp.repeat(heights, shape[axis_at] // blocks).reshape([-1 if axis == axis_at else 1 for axis in range(len(shape))])
    return gain


def centred(key, shape, deviation, most, cuts=(), kind=jnp.bfloat16):
    drawn = deviation * jax.random.normal(key, shape, jnp.float32)
    if cuts:
        drawn = drawn * steps_of(key, shape, cuts, -0.22, 0.18)
    return jnp.clip(drawn, -most, most).astype(kind)


def setup_inputs(seed: int = 0) -> dict:
    arg_keys = jax.random.split(jax.random.key(seed), 15)
    tool_len = draw_tool_len(jax.random.fold_in(arg_keys[14], 71), 0)
    state_table = draw_state_table(jax.random.fold_in(arg_keys[14], 71), 0)
    page_table = draw_page_table(jax.random.fold_in(arg_keys[14], 71), 0)
    kda_pool = centred(arg_keys[3], (HEADS, SSLOTS, HD, HD), 1.0, 6.0, ((0, 8), (1, 64)))
    latent_pool = centred(arg_keys[4], (CLASSES, PSLOTS, PAGE, LAT), 1.0, 6.0, ((0, 8), (1, 64)))
    kda_q = centred(arg_keys[5], (ROWS, CALLOUT_POSITIONS, HEADS * HD), 1.0, 6.0, ((0, 64), (2, 8)))
    kda_k = centred(arg_keys[6], (ROWS, CALLOUT_POSITIONS, HEADS * HD), 1.0, 6.0, ((0, 64), (2, 8)))
    kda_v = centred(arg_keys[7], (ROWS, CALLOUT_POSITIONS, HEADS * HD), 1.0, 6.0, ((0, 64), (2, 8)))
    kda_gate = draw_kda_gate(jax.random.fold_in(arg_keys[14], 71), 0)
    kda_beta = centred(arg_keys[9], (ROWS, CALLOUT_POSITIONS, HEADS), 1.5, 6.0, ((0, 64), (2, 8)))
    mla_q = draw_mla_q(jax.random.fold_in(arg_keys[14], 71), 0)
    mla_new = centred(arg_keys[11], (ROWS, CALLOUT_POSITIONS, LAT), 1.0, 6.0, ((0, 64),))
    w_uk = centred(arg_keys[12], (HEADS, HD, LAT), HD ** -0.5, 0.5, ((0, 8),))
    w_uv = centred(arg_keys[13], (HEADS, LAT, HD), LAT ** -0.5, 0.25, ((0, 8),))
    return dict(tool_len=tool_len, state_table=state_table, page_table=page_table, kda_pool=kda_pool, latent_pool=latent_pool, kda_q=kda_q, kda_k=kda_k, kda_v=kda_v, kda_gate=kda_gate, kda_beta=kda_beta, mla_q=mla_q, mla_new=mla_new, w_uk=w_uk, w_uv=w_uv)


EPSILON = 1e-06
HIGHEST = lax.Precision.HIGHEST

def unit_norm(values):
    return values / jnp.sqrt(lax.optimization_barrier(jnp.sum(values * values, axis=-1, keepdims=True)) + EPSILON)

def through_bf16(values):
    return lax.optimization_barrier(values.astype(jnp.bfloat16)).astype(jnp.float32)

def reference(tool_len, state_table, page_table, kda_pool, latent_pool, kda_q, kda_k, kda_v, kda_gate, kda_beta, mla_q, mla_new, w_uk, w_uv):
    sequence_count = tool_len.shape[0]
    row_groups = sequence_count // ROWS_DEV
    head_ids = jnp.arange(HEADS)
    class_ids = jnp.arange(CLASSES)
    up_keys = w_uk.astype(jnp.float32)
    up_values = w_uv.astype(jnp.float32)
    positions = jnp.arange(CALLOUT_POSITIONS)
    causal = (positions[None, :] <= positions[:, None])[None, :, None, :]

    def grouped(values):
        return values.reshape((row_groups, ROWS_DEV) + values.shape[1:])

    def per_head(values):
        return values.reshape(ROWS_DEV, CALLOUT_POSITIONS, HEADS, HD).astype(jnp.float32)

    def one_group(items):
        lengths, slots, page_ids, queries, keys_in, values_in, gates, beta_in, lat_queries, fresh = items
        alive = (positions[None, :] < lengths[:, None]).astype(jnp.float32)
        state = kda_pool[head_ids[None, :], slots].astype(jnp.float32)
        query_n = unit_norm(per_head(queries))
        key_n = unit_norm(per_head(keys_in))
        value_f = per_head(values_in)
        betas = jax.nn.sigmoid(beta_in.astype(jnp.float32)) * alive[:, :, None]
        decays = jnp.exp(per_head(gates) * alive[:, :, None, None])

        def step(carry, inputs):
            q_now, k_now, v_now, b_now, d_now = inputs
            kept = d_now[..., None] * carry
            seen = jnp.einsum('rhc,rhcd->rhd', k_now, kept, precision=HIGHEST)
            update = b_now[..., None] * (v_now - seen)
            carry = kept + k_now[..., None] * update[..., None, :]
            return (carry, jnp.einsum('rhc,rhcd->rhd', q_now, carry, precision=HIGHEST))

        def swap(values):
            return jnp.swapaxes(values, 0, 1)
        _, outputs = lax.scan(step, state, (swap(query_n), swap(key_n), swap(value_f), swap(betas), swap(decays)))
        kda_rows = (swap(outputs) * alive[:, :, None, None]).reshape(ROWS_DEV, CALLOUT_POSITIONS, HEADS * HD).astype(jnp.bfloat16)
        context = latent_pool[class_ids[None, :, None], page_ids]
        context = context.reshape(ROWS_DEV, CTX, LAT).astype(jnp.float32)
        lifted = through_bf16(jnp.einsum('rthd,hdl->rthl', per_head(lat_queries), up_keys, precision=HIGHEST))
        scale = HD ** (-0.5)
        fresh_f = fresh.astype(jnp.float32)
        old_scores = jnp.einsum('rthl,rcl->rthc', lifted, context, precision=HIGHEST) * scale
        new_scores = jnp.einsum('rthl,rsl->rths', lifted, fresh_f, precision=HIGHEST) * scale
        new_scores = jnp.where(causal, new_scores, -1e+30)
        top = jnp.maximum(lax.optimization_barrier(jnp.max(old_scores, axis=-1)), lax.optimization_barrier(jnp.max(new_scores, axis=-1)))
        old_e = jnp.exp(old_scores - top[..., None])
        new_e = jnp.where(causal, jnp.exp(new_scores - top[..., None]), 0.0)
        totals = lax.optimization_barrier(jnp.sum(old_e, axis=-1)) + lax.optimization_barrier(jnp.sum(new_e, axis=-1))
        mixed = jnp.einsum('rthc,rcl->rthl', through_bf16(old_e), context, precision=HIGHEST)
        mixed = mixed + jnp.einsum('rths,rsl->rthl', through_bf16(new_e), fresh_f, precision=HIGHEST)
        attended = through_bf16(mixed / totals[..., None])
        result = jnp.einsum('rthl,hld->rthd', attended, up_values, precision=HIGHEST) * alive[:, :, None, None]
        mla_rows = result.reshape(ROWS_DEV, CALLOUT_POSITIONS, HEADS * HD).astype(jnp.bfloat16)
        return (kda_rows, mla_rows)
    kda_all, mla_all = lax.map(one_group, (grouped(tool_len), grouped(state_table), grouped(page_table), grouped(kda_q), grouped(kda_k), grouped(kda_v), grouped(kda_gate), grouped(kda_beta), grouped(mla_q), grouped(mla_new)))
    return (kda_all.reshape(sequence_count, CALLOUT_POSITIONS, HEADS * HD), mla_all.reshape(sequence_count, CALLOUT_POSITIONS, HEADS * HD))
```

```python
import functools

import jax
import jax.numpy as jnp
from jax import lax
from jax.experimental import pallas as pl
from jax.experimental.pallas import tpu as pltpu
from jax.sharding import PartitionSpec as P

EPSILON = 1e-06
F32 = jnp.float32
BF16 = jnp.bfloat16


def mm(a, b):
    return lax.dot_general(a, b, (((1,), (0,)), ((), ())), preferred_element_type=F32)


def mm_nt(a, b):
    return lax.dot_general(a, b, (((1,), (1,)), ((), ())), preferred_element_type=F32)


def halves(values):
    high = values.astype(BF16)
    return high, (values - high.astype(F32)).astype(BF16)


def mm3(a, b, dot=mm):
    a_high, a_low = halves(a)
    b_high, b_low = halves(b)
    return dot(a_high, b_high) + (dot(a_high, b_low) + dot(a_low, b_high))


def unit_norm(values):
    return values / jnp.sqrt(jnp.sum(values * values, axis=-1, keepdims=True) + EPSILON)


def stack_heads(block, heads, width):
    return jnp.concatenate([block[:, h * width : (h + 1) * width] for h in range(heads)], axis=0)


def recall_coefficients(queries, keys, values, gates, betas, alive, tokens):
    rows = queries.shape[0]
    later = lax.broadcasted_iota(jnp.int32, (rows, rows), 0)
    sooner = lax.broadcasted_iota(jnp.int32, (rows, rows), 1)
    same = (later // tokens) == (sooner // tokens)
    reached = same & (sooner <= later)
    summed = mm(reached.astype(F32).astype(BF16), (gates.astype(F32) * alive).astype(BF16))
    grown = jnp.exp(summed)
    key_n = unit_norm(keys.astype(F32))
    query_up = unit_norm(queries.astype(F32)) * grown
    key_up = key_n * grown
    key_down = key_n * jnp.exp(-summed)
    mixing = mm3(key_up, key_down, mm_nt) * betas
    reach = jnp.where(reached, mm3(query_up, key_down, mm_nt), 0.0)
    inverse = (later == sooner).astype(F32)
    size = 1
    while size < tokens:
        pair = 2 * size
        corner = ((later // pair) == (sooner // pair)) & (later % pair >= size) & (sooner % pair < size)
        part = jnp.where(corner, mixing, 0.0)
        if size == 1:
            inverse = inverse - part
        else:
            inverse = inverse - mm3(mm3(inverse, part), inverse)
        size = pair
    spread = mm3(reach, inverse)
    coefficient = query_up - mm3(spread, betas * key_up)
    offset = mm3(spread, betas * values.astype(F32))
    return coefficient, offset


def fused(
    sizes,
    picked_ref,
    slot_ref,
    len_ref,
    states_ref,
    pages_ref,
    q_ref,
    k_ref,
    v_ref,
    gate_ref,
    beta_ref,
    mq_ref,
    new_ref,
    wuk_ref,
    wuv_ref,
    recall_ref,
    mla_ref,
    records,
    outgoing,
    incoming,
    lift_out,
    lift_in,
    wuv_in,
    page_out,
    context,
    result_out,
    coefs,
    offsets,
    x_send_sem,
    x_recv_sem,
    swap_send_sem,
    swap_recv_sem,
    lift_send_sem,
    lift_recv_sem,
    wuv_send_sem,
    wuv_recv_sem,
    back_send_sem,
    back_recv_sem,
):
    n_dp, n_t, cap = sizes
    heads, slots, hd, _ = states_ref.shape
    page_len, latent = pages_ref.shape[2], pages_ref.shape[3]
    rows, tokens, _ = q_ref.shape
    folds = latent // hd
    me = lax.axis_index("dp")
    mine = lax.axis_index("tensor")

    barrier = pltpu.get_barrier_semaphore()

    def greet_dp(k, c):
        pl.semaphore_signal(barrier, inc=1, device_id={"dp": (me + k) % n_dp})
        return c

    def greet_tensor(k, c):
        pl.semaphore_signal(barrier, inc=1, device_id={"tensor": (mine + k) % n_t})
        return c

    lax.fori_loop(1, n_dp, greet_dp, 0)
    lax.fori_loop(1, n_t, greet_tensor, 0)

    def put_state(i, c):
        records[i] = states_ref[i // slots, i % slots]
        return c

    def put_page(i, c):
        page = pages_ref[0, i]
        for f in range(folds):
            records[heads * slots + i, f * page_len : (f + 1) * page_len, :] = page[
                :, f * hd : (f + 1) * hd
            ]
        return c

    lax.fori_loop(0, heads * slots, put_state, 0)
    lax.fori_loop(0, pages_ref.shape[1], put_page, 0)
    for s in range(cap):
        incoming[me * cap + s] = records[picked_ref[me * cap + s]]

    pl.semaphore_wait(barrier, n_dp + n_t - 2)

    def send_records(k, c):
        peer = (me + (k * 27) % n_dp) % n_dp
        for s in range(cap):
            outgoing[peer * cap + s] = records[picked_ref[peer * cap + s]]
        pltpu.make_async_remote_copy(
            src_ref=outgoing.at[pl.ds(peer * cap, cap)],
            dst_ref=incoming.at[pl.ds(me * cap, cap)],
            send_sem=x_send_sem,
            recv_sem=x_recv_sem,
            device_id={"dp": peer},
        ).start()
        return c

    lax.fori_loop(1, n_dp, send_records, 0)

    for h in range(heads):
        queries = mq_ref[:, :, h * hd : (h + 1) * hd].reshape(rows * tokens, hd)
        lifted = mm(queries, wuk_ref[h]).astype(BF16)
        lift_out[:, h] = lifted.reshape(rows, tokens, latent)
    lift_in[0] = lift_out[mine]
    wuv_in[0] = wuv_ref[...]

    def lift_copy(k):
        peer = (mine + k) % n_t
        return pltpu.make_async_remote_copy(
            src_ref=lift_out.at[peer],
            dst_ref=lift_in.at[n_t - k],
            send_sem=lift_send_sem.at[k],
            recv_sem=lift_recv_sem.at[n_t - k],
            device_id={"tensor": peer},
        )

    def wuv_copy(k):
        peer = (mine + k) % n_t
        return pltpu.make_async_remote_copy(
            src_ref=wuv_ref,
            dst_ref=wuv_in.at[n_t - k],
            send_sem=wuv_send_sem.at[k],
            recv_sem=wuv_recv_sem.at[n_t - k],
            device_id={"tensor": peer},
        )

    def page_copy(k):
        peer = (mine + k) % n_t
        return pltpu.make_async_remote_copy(
            src_ref=page_out.at[peer],
            dst_ref=context.at[n_t - k],
            send_sem=swap_send_sem.at[k],
            recv_sem=swap_recv_sem.at[n_t - k],
            device_id={"tensor": peer},
        )

    def back_copy(k):
        peer = (mine + k) % n_t
        return pltpu.make_async_remote_copy(
            src_ref=result_out.at[k],
            dst_ref=mla_ref.at[mine],
            send_sem=back_send_sem.at[k],
            recv_sem=back_recv_sem.at[n_t - k],
            device_id={"tensor": peer},
        )

    for k in range(1, n_t):
        lift_copy(k).start()
    for k in range(1, n_t):
        wuv_copy(k).start()

    def make_coefficients(r, c):
        alive = (
            lax.broadcasted_iota(jnp.int32, (heads * tokens, 1), 0) % tokens < len_ref[r]
        ).astype(F32)
        raw = beta_ref[r].astype(F32)
        betas = jnp.concatenate([raw[:, h : h + 1] for h in range(heads)], axis=0)
        betas = alive / (1.0 + jnp.exp(-betas))
        coefficient, offset = recall_coefficients(
            stack_heads(q_ref[r], heads, hd),
            stack_heads(k_ref[r], heads, hd),
            stack_heads(v_ref[r], heads, hd),
            stack_heads(gate_ref[r], heads, hd),
            betas,
            alive,
            tokens,
        )
        coefs[r] = coefficient
        offsets[r] = offset
        return c

    lax.fori_loop(0, rows, make_coefficients, 0)

    fresh = new_ref[mine]
    context[n_t] = jnp.concatenate(
        [fresh, jnp.zeros((context.shape[1] - tokens, latent), BF16)], axis=0
    )

    away = (n_dp - 1) * cap
    pltpu.make_async_copy(
        incoming.at[pl.ds(0, away)], incoming.at[pl.ds(0, away)], x_recv_sem
    ).wait()

    n_states = heads * rows

    def place_page(i, c):
        record = incoming[slot_ref[n_states + i]]
        for f in range(folds):
            page_out[
                i // pages_row,
                pl.ds((i % pages_row) * page_len, page_len),
                f * hd : (f + 1) * hd,
            ] = record[f * page_len : (f + 1) * page_len]
        return c

    pages_row = page_out.shape[1] // page_len
    lax.fori_loop(0, rows * pages_row, place_page, 0)
    context[0] = page_out[mine]
    for k in range(1, n_t):
        page_copy(k).start()

    def recall(r, c):
        alive = (lax.broadcasted_iota(jnp.int32, (tokens, 1), 0) < len_ref[r]).astype(F32)
        for h in range(heads):
            state = incoming[slot_ref[h * rows + r]]
            high, low = halves(coefs[r, h * tokens : (h + 1) * tokens, :])
            both = mm(jnp.concatenate([high, low], axis=0), state)
            seen = both[:tokens] + both[tokens:] + offsets[r, h * tokens : (h + 1) * tokens, :]
            recall_ref[r, :, h * hd : (h + 1) * hd] = (seen * alive).astype(BF16)
        return c

    lax.fori_loop(0, rows, recall, 0)

    for k in range(1, n_t):
        lift_copy(k).wait_recv()
        wuv_copy(k).wait_recv()
    for k in range(1, n_t):
        page_copy(k).wait_recv()

    every = heads * tokens
    scale = hd ** (-0.5)
    total_keys = context.shape[0] * context.shape[1]
    old_keys = n_t * context.shape[1]
    column = lax.broadcasted_iota(jnp.int32, (every, total_keys), 1) - old_keys
    token = lax.broadcasted_iota(jnp.int32, (every, total_keys), 0) % tokens
    row_alive = (lax.broadcasted_iota(jnp.int32, (tokens, 1), 0) < len_ref[mine]).astype(F32)

    def attend(k):
        keys = context[...].reshape(total_keys, latent)
        queries = lift_in[k].reshape(every, latent)
        scores = mm_nt(queries, keys) * scale
        scores = jnp.where(column <= token, scores, -1e30)
        top = jnp.max(scores, axis=-1, keepdims=True)
        e = jnp.exp(scores - top)
        total = jnp.sum(e, axis=-1, keepdims=True)
        mixed = mm(e.astype(BF16), keys)
        attended = (mixed / total).astype(BF16)
        for h in range(heads):
            out = mm(attended[h * tokens : (h + 1) * tokens], wuv_in[k, h]) * row_alive
            result_out[k, :, h * hd : (h + 1) * hd] = out.astype(BF16)

    def attend_away(k, c):
        attend(k)
        back_copy(k).start()
        return c

    lax.fori_loop(1, n_t, attend_away, 0)
    attend(0)
    mla_ref[mine] = result_out[0]

    for k in range(1, n_t):
        back_copy(k).wait_recv()
    for k in range(1, n_t):
        lift_copy(k).wait_send()
        wuv_copy(k).wait_send()
        page_copy(k).wait_send()
        back_copy(k).wait_send()
    pltpu.make_async_copy(
        outgoing.at[pl.ds(0, away)], outgoing.at[pl.ds(0, away)], x_send_sem
    ).wait()


def run_fused(
    n_dp,
    n_t,
    cap,
    picked,
    slot,
    tool_len,
    kda_pool,
    latent_pool,
    kda_q,
    kda_k,
    kda_v,
    kda_gate,
    kda_beta,
    mla_q,
    mla_new,
    w_uk,
    w_uv,
):
    heads, slots, hd, _ = kda_pool.shape
    _, pool_pages, page_len, latent = latent_pool.shape
    rows, tokens, _ = kda_q.shape
    pages_row = pool_pages // rows
    vmem = pl.BlockSpec(memory_space=pltpu.VMEM)
    smem = pl.BlockSpec(memory_space=pltpu.SMEM)
    out = jax.ShapeDtypeStruct(kda_q.shape, BF16)
    dma = pltpu.SemaphoreType.DMA
    return pl.pallas_call(
        functools.partial(fused, (n_dp, n_t, cap)),
        out_shape=(out, out),
        in_specs=[smem] * 3 + [vmem] * 11,
        out_specs=(vmem, vmem),
        scratch_shapes=[
            pltpu.VMEM((heads * slots + pool_pages, hd, hd), BF16),
            pltpu.VMEM((n_dp * cap, hd, hd), BF16),
            pltpu.VMEM((n_dp * cap, hd, hd), BF16),
            pltpu.VMEM((rows, heads, tokens, latent), BF16),
            pltpu.VMEM((n_t, heads, tokens, latent), BF16),
            pltpu.VMEM((n_t, heads, latent, hd), BF16),
            pltpu.VMEM((rows, pages_row * page_len, latent), BF16),
            pltpu.VMEM((n_t + 1, pages_row * page_len, latent), BF16),
            pltpu.VMEM((n_t, tokens, heads * hd), BF16),
            pltpu.VMEM((rows, heads * tokens, hd), F32),
            pltpu.VMEM((rows, heads * tokens, hd), F32),
            dma,
            dma,
        ]
        + [dma((n_t,))] * 8,
        compiler_params=pltpu.CompilerParams(
            collective_id=0, has_side_effects=True, vmem_limit_bytes=48 * 1024 * 1024
        ),
    )(
        picked,
        slot,
        tool_len,
        kda_pool,
        latent_pool,
        kda_q,
        kda_k,
        kda_v,
        kda_gate,
        kda_beta,
        mla_q,
        mla_new,
        w_uk,
        w_uv,
    )


def routes(state_table, page_table, n_dp, heads, rows, pool_pages):
    me = lax.axis_index("dp")
    mine = lax.axis_index("tensor")
    pages_row = page_table.shape[2]
    states = lax.dynamic_slice_in_dim(state_table, mine * heads, heads, 1).T
    pages = lax.dynamic_index_in_dim(page_table, mine, 1, keepdims=False).T
    owners = jnp.concatenate([states // rows, pages // pool_pages], axis=0)
    head = lax.broadcasted_iota(jnp.int32, states.shape, 0)
    ids = jnp.concatenate([head * rows + states % rows, heads * rows + pages % pool_pages], axis=0)
    kinds = heads + pages_row
    here = (owners == me).reshape(kinds, n_dp, rows)
    ids3 = ids.reshape(kinds, n_dp, rows)
    top = heads * rows + pool_pages - 1
    first = jnp.min(jnp.where(here, ids3, top), axis=(0, 2))
    second = jnp.max(jnp.where(here, ids3, 0), axis=(0, 2))
    picked = jnp.stack([first, second], axis=1).reshape(-1)
    own = lax.dynamic_slice_in_dim(owners, me * rows, rows, 1)
    own_ids = lax.dynamic_slice_in_dim(ids, me * rows, rows, 1)
    own = jnp.concatenate([own[:heads].reshape(-1), own[heads:].T.reshape(-1)])
    own_ids = jnp.concatenate([own_ids[:heads].reshape(-1), own_ids[heads:].T.reshape(-1)])
    behind = (own[None, :] == own[:, None]) & (own_ids[None, :] < own_ids[:, None])
    slot = 2 * own + jnp.any(behind, axis=1).astype(jnp.int32)
    return picked, slot


def local(
    tool_len,
    state_table,
    page_table,
    kda_pool,
    latent_pool,
    kda_q,
    kda_k,
    kda_v,
    kda_gate,
    kda_beta,
    mla_q,
    mla_new,
    w_uk,
    w_uv,
):
    n_dp, n_t = lax.axis_size("dp"), lax.axis_size("tensor")
    picked, slot = routes(
        state_table, page_table, n_dp, kda_pool.shape[0], tool_len.shape[0], latent_pool.shape[1]
    )
    return run_fused(
        n_dp,
        n_t,
        2,
        picked,
        slot,
        tool_len,
        kda_pool,
        latent_pool,
        kda_q,
        kda_k,
        kda_v,
        kda_gate,
        kda_beta,
        mla_q,
        mla_new,
        w_uk,
        w_uv,
    )


def solution(mesh):
    in_specs = (
        P("dp"),
        P(),
        P(),
        P("tensor", "dp", None, None),
        P("tensor", "dp", None, None),
        P("dp", None, "tensor"),
        P("dp", None, "tensor"),
        P("dp", None, "tensor"),
        P("dp", None, "tensor"),
        P("dp", None, "tensor"),
        P("dp", None, "tensor"),
        P("dp", None, None),
        P("tensor", None, None),
        P("tensor", None, None),
    )
    out_specs = (P("dp", None, "tensor"), P("dp", None, "tensor"))
    return jax.shard_map(local, mesh=mesh, in_specs=in_specs, out_specs=out_specs, check_vma=False)
```

```python
import functools

import jax
import jax.numpy as jnp
from jax import lax
from jax.experimental import pallas as pl
from jax.experimental.pallas import tpu as pltpu
from jax.sharding import PartitionSpec as P

EPSILON = 1e-06
F32 = jnp.float32
BF16 = jnp.bfloat16
LANES = 128
SIDE_Y = 8


def mm(a, b):
    return lax.dot_general(a, b, (((1,), (0,)), ((), ())), preferred_element_type=F32)


def mm_nt(a, b):
    return lax.dot_general(a, b, (((1,), (1,)), ((), ())), preferred_element_type=F32)


def halves(values):
    high = values.astype(BF16)
    return high, (values - high.astype(F32)).astype(BF16)


def mm3(a, b, dot=mm):
    a_high, a_low = halves(a)
    b_high, b_low = halves(b)
    return dot(a_high, b_high) + (dot(a_high, b_low) + dot(a_low, b_high))


def unit_norm(values):
    return values / jnp.sqrt(jnp.sum(values * values, axis=-1, keepdims=True) + EPSILON)


def stack_heads(block, heads, width):
    return jnp.concatenate([block[:, h * width : (h + 1) * width] for h in range(heads)], axis=0)


def recall_coefficients(queries, keys, values, gates, betas, alive, tokens):
    rows = queries.shape[0]
    later = lax.broadcasted_iota(jnp.int32, (rows, rows), 0)
    sooner = lax.broadcasted_iota(jnp.int32, (rows, rows), 1)
    same = (later // tokens) == (sooner // tokens)
    reached = same & (sooner <= later)
    summed = mm(reached.astype(F32).astype(BF16), (gates.astype(F32) * alive).astype(BF16))
    grown = jnp.exp(summed)
    key_n = unit_norm(keys.astype(F32))
    query_up = unit_norm(queries.astype(F32)) * grown
    key_up = key_n * grown
    key_down = key_n * jnp.exp(-summed)
    mixing = mm3(key_up, key_down, mm_nt) * betas
    reach = jnp.where(reached, mm3(query_up, key_down, mm_nt), 0.0)
    inverse = (later == sooner).astype(F32)
    size = 1
    while size < tokens:
        pair = 2 * size
        corner = ((later // pair) == (sooner // pair)) & (later % pair >= size) & (sooner % pair < size)
        part = jnp.where(corner, mixing, 0.0)
        if size == 1:
            inverse = inverse - part
        else:
            inverse = inverse - mm3(mm3(inverse, part), inverse)
        size = pair
    spread = mm3(reach, inverse)
    coefficient = query_up - mm3(spread, betas * key_up)
    offset = mm3(spread, betas * values.astype(F32))
    return coefficient, offset


def routes(states, pages, me, side, rows, slots, pool_pages):
    n_z, n_y = side
    n_dp = n_z * n_y
    heads = states.shape[0]
    lanes = states.shape[1]
    kinds = heads + pages.shape[0]
    owners = jnp.concatenate([states // slots, pages // pool_pages], axis=0)
    head = lax.broadcasted_iota(jnp.int32, states.shape, 0)
    ids = jnp.concatenate(
        [head * slots + states % slots, heads * slots + pages % pool_pages], axis=0
    )
    here = owners == me
    first = jnp.min(jnp.where(here, ids, heads * slots + pool_pages - 1), axis=0, keepdims=True)
    second = jnp.max(jnp.where(here, ids, 0), axis=0, keepdims=True)
    span = 1
    while span < rows:
        first = jnp.minimum(first, pltpu.roll(first, lanes - span, 1))
        second = jnp.maximum(second, pltpu.roll(second, lanes - span, 1))
        span *= 2
    keys = owners * (heads * slots + pool_pages) + ids
    own = pltpu.roll(keys, (lanes - me * rows) % lanes, 1)[:, :LANES]
    place = lax.broadcasted_iota(jnp.int32, (1, LANES), 1)
    flat = jnp.zeros((1, LANES), jnp.int32)
    for kind in range(kinds):
        row = own[kind : kind + 1]
        if kind:
            row = pltpu.roll(row, kind * rows, 1)
        flat = jnp.where(place // rows == kind, row, flat)
    across = jnp.broadcast_to(flat, (LANES, LANES))
    down = jnp.transpose(across.astype(F32)).astype(jnp.int32)
    base = heads * slots + pool_pages
    valid = lax.broadcasted_iota(jnp.int32, (LANES, LANES), 0) < kinds * rows
    behind = valid & (down // base == across // base) & (down < across)
    late = jnp.max(behind.astype(F32), axis=0, keepdims=True).astype(jnp.int32)
    source = flat // base
    over_z = (me // n_y - source // n_y + n_z) % n_z
    over_y = (me % n_y - source % n_y + n_y) % n_y
    by_z = jnp.where(over_y == 0, 0, n_dp) + over_z * n_y + over_y
    by_y = jnp.where(over_z == 0, 0, n_dp) + over_y * n_z + over_z + 2 * n_dp
    return first, second, jnp.where(late == 0, by_z, by_y)


def fused(
    sizes,
    len_ref,
    state_table_ref,
    page_table_ref,
    states_ref,
    pages_ref,
    q_ref,
    k_ref,
    v_ref,
    gate_ref,
    beta_ref,
    mq_ref,
    new_ref,
    wuk_ref,
    wuv_ref,
    recall_ref,
    mla_ref,
    records,
    q_buf,
    k_buf,
    v_buf,
    gate_buf,
    beta_buf,
    mq_buf,
    new_buf,
    wuk_buf,
    wuv_buf,
    state_slots,
    page_slots,
    picked_rows,
    place_row,
    picked,
    place,
    outgoing,
    incoming,
    lift_out,
    lift_in,
    wuv_in,
    page_out,
    context,
    result_out,
    coefs,
    offsets,
    send_sem,
    first_sem,
    second_sem,
    swap_send_sem,
    swap_recv_sem,
    lift_send_sem,
    lift_recv_sem,
    wuv_send_sem,
    wuv_recv_sem,
    back_send_sem,
    back_recv_sem,
    record_sem,
    load_sem,
    table_sem,
):
    n_z, n_y, n_t = sizes
    n_dp = n_z * n_y
    side = (n_z, n_y)
    heads, slots, hd, _ = states_ref.shape
    page_len, latent = pages_ref.shape[2], pages_ref.shape[3]
    rows, tokens, _ = q_ref.shape
    folds = latent // hd
    me = lax.axis_index("dp")
    mine = lax.axis_index("tensor")
    at_z, at_y = me // n_y, me % n_y

    n_local = heads * slots
    record_loads = [
        pltpu.make_async_copy(
            states_ref.at[h], records.at[pl.ds(h * slots, slots)], record_sem.at[h]
        )
        for h in range(heads)
    ] + [
        pltpu.make_async_copy(
            pages_ref.at[0, :, :, f * hd : (f + 1) * hd],
            records.at[pl.ds(n_local, pages_ref.shape[1]), f * page_len : (f + 1) * page_len, :],
            record_sem.at[heads + f],
        )
        for f in range(folds)
    ]
    loads = [
        pltpu.make_async_copy(source, target, load_sem.at[i])
        for i, (source, target) in enumerate(
            (
                (mq_ref, mq_buf),
                (wuk_ref, wuk_buf),
                (wuv_ref, wuv_buf),
                (q_ref, q_buf),
                (k_ref, k_buf),
                (v_ref, v_buf),
                (gate_ref, gate_buf),
                (beta_ref, beta_buf),
                (new_ref, new_buf),
            )
        )
    ]
    table_loads = [
        pltpu.make_async_copy(state_table_ref, state_slots, table_sem.at[0]),
        pltpu.make_async_copy(page_table_ref.at[mine], page_slots, table_sem.at[1]),
    ]
    for load in table_loads + record_loads + loads:
        load.start()

    barrier = pltpu.get_barrier_semaphore()

    def greet_z(k, c):
        pl.semaphore_signal(barrier, inc=1, device_id={"dp": ((at_z + k) % n_z) * n_y + at_y})
        return c

    def greet_y(k, c):
        pl.semaphore_signal(barrier, inc=1, device_id={"dp": at_z * n_y + (at_y + k) % n_y})
        return c

    def greet_tensor(k, c):
        pl.semaphore_signal(barrier, inc=1, device_id={"tensor": (mine + k) % n_t})
        return c

    lax.fori_loop(1, n_z, greet_z, 0)
    lax.fori_loop(1, n_y, greet_y, 0)
    lax.fori_loop(1, n_t, greet_tensor, 0)

    for load in table_loads:
        load.wait()
    mine_slots = state_slots[0:heads, :]
    for t in range(1, n_t):
        mine_slots = jnp.where(mine == t, state_slots[t * heads : (t + 1) * heads, :], mine_slots)
    first, second, slot = routes(
        mine_slots,
        page_slots[...],
        me,
        (n_z, n_y),
        rows,
        slots,
        pages_ref.shape[1],
    )
    picked_rows[0:1, :] = first
    picked_rows[1:2, :] = second
    place_row[...] = slot
    scalars = [
        pltpu.make_async_copy(picked_rows, picked, table_sem.at[2]),
        pltpu.make_async_copy(place_row, place, table_sem.at[3]),
    ]
    for load in scalars:
        load.start()
    for load in scalars + record_loads:
        load.wait()

    def hop(which, leg, k):
        along_z = which == leg
        if along_z:
            return {"dp": ((at_z + k) % n_z) * n_y + at_y}
        return {"dp": at_z * n_y + (at_y + k) % n_y}

    def stage(which, k, j):
        over_z, over_y = (k, j) if which == 0 else (j, k)
        target = ((at_z + over_z) % n_z) * n_y + (at_y + over_y) % n_y
        return records[picked[which, target * rows]]

    def nearest(i, n):
        return (((i + 1) // 2) * (1 - 2 * ((i + 1) % 2)) + n) % n

    def spot(which, leg, k, j):
        return ((2 * which + leg) * side[which] + k) * side[1 - which] + j

    def first_leg(which, k):
        return pltpu.make_async_remote_copy(
            src_ref=outgoing.at[which, k],
            dst_ref=incoming.at[pl.ds(spot(which, 0, k, 0), side[1 - which])],
            send_sem=send_sem.at[which, 0, k],
            recv_sem=first_sem.at[which, k],
            device_id=hop(which, 0, k),
        )

    def second_leg(which, k, j, own):
        held = outgoing.at[which, k, j] if own else incoming.at[spot(which, 0, k, j)]
        return pltpu.make_async_remote_copy(
            src_ref=held,
            dst_ref=incoming.at[spot(which, 1, k, j)],
            send_sem=send_sem.at[which, 1, j],
            recv_sem=second_sem.at[which, j],
            device_id=hop(which, 1, j),
        )

    def forward(which, k, own):
        n = side[1 - which]

        def one(i, c):
            second_leg(which, k, nearest(i, n), own).start()
            return c

        lax.fori_loop(1, n, one, 0)

    for which in range(2):
        incoming[spot(which, 0, 0, 0)] = stage(which, 0, 0)

    pl.semaphore_wait(barrier, n_z + n_y + n_t - 3)

    def send_first(which, k):
        for j in range(side[1 - which]):
            outgoing[which, k, j] = stage(which, k, j)
        first_leg(which, k).start()

    for i in range(1, max(side)):
        for which in range(2):
            if i < side[which]:
                send_first(which, nearest(i, side[which]))
    for which in range(2):
        for j in range(1, side[1 - which]):
            outgoing[which, 0, j] = stage(which, 0, j)
        forward(which, 0, True)

    for load in loads:
        load.wait()

    for h in range(heads):
        queries = mq_buf[:, :, h * hd : (h + 1) * hd].reshape(rows * tokens, hd)
        lifted = mm(queries, wuk_buf[h]).astype(BF16)
        lift_out[:, h] = lifted.reshape(rows, tokens, latent)
    lift_in[0] = lift_out[mine]
    wuv_in[0] = wuv_buf[...]

    def lift_copy(k):
        peer = (mine + k) % n_t
        return pltpu.make_async_remote_copy(
            src_ref=lift_out.at[peer],
            dst_ref=lift_in.at[n_t - k],
            send_sem=lift_send_sem.at[k],
            recv_sem=lift_recv_sem.at[n_t - k],
            device_id={"tensor": peer},
        )

    def wuv_copy(k):
        peer = (mine + k) % n_t
        return pltpu.make_async_remote_copy(
            src_ref=wuv_buf,
            dst_ref=wuv_in.at[n_t - k],
            send_sem=wuv_send_sem.at[k],
            recv_sem=wuv_recv_sem.at[n_t - k],
            device_id={"tensor": peer},
        )

    def page_copy(k):
        peer = (mine + k) % n_t
        return pltpu.make_async_remote_copy(
            src_ref=page_out.at[peer],
            dst_ref=context.at[n_t - k],
            send_sem=swap_send_sem.at[k],
            recv_sem=swap_recv_sem.at[n_t - k],
            device_id={"tensor": peer},
        )

    def back_copy(k):
        peer = (mine + k) % n_t
        return pltpu.make_async_remote_copy(
            src_ref=result_out.at[k],
            dst_ref=mla_ref.at[mine],
            send_sem=back_send_sem.at[k],
            recv_sem=back_recv_sem.at[n_t - k],
            device_id={"tensor": peer},
        )

    for k in range(1, n_t):
        lift_copy(k).start()
    for k in range(1, n_t):
        wuv_copy(k).start()

    def make_coefficients(r, c):
        alive = (
            lax.broadcasted_iota(jnp.int32, (heads * tokens, 1), 0) % tokens < len_ref[r]
        ).astype(F32)
        raw = beta_buf[r].astype(F32)
        betas = jnp.concatenate([raw[:, h : h + 1] for h in range(heads)], axis=0)
        betas = alive / (1.0 + jnp.exp(-betas))
        coefficient, offset = recall_coefficients(
            stack_heads(q_buf[r], heads, hd),
            stack_heads(k_buf[r], heads, hd),
            stack_heads(v_buf[r], heads, hd),
            stack_heads(gate_buf[r], heads, hd),
            betas,
            alive,
            tokens,
        )
        coefs[r] = coefficient
        offsets[r] = offset
        return c

    def pass_on(i, c):
        for which in range(2):
            k = nearest(i, side[which])
            first_leg(which, k).wait_recv()
            forward(which, k, False)
        return c

    def work(i, c):
        make_coefficients(i - 1, c)
        return pass_on(i, c)

    assert n_z == n_y
    paired = min(rows, n_z - 1)
    lax.fori_loop(1, paired + 1, work, 0)
    lax.fori_loop(paired + 1, n_z, pass_on, 0)
    lax.fori_loop(paired, rows, make_coefficients, 0)

    fresh = new_buf[mine]
    context[n_t] = jnp.concatenate(
        [fresh, jnp.zeros((context.shape[1] - tokens, latent), BF16)], axis=0
    )

    for which in range(2):
        for j in range(1, side[1 - which]):
            column = incoming.at[pl.ds(spot(which, 1, 0, 0), side[which])]
            pltpu.make_async_copy(column, column, second_sem.at[which, j]).wait()

    n_states = heads * rows

    def place_page(i, c):
        record = incoming[place[0, n_states + (i % pages_row) * rows + i // pages_row]]
        for f in range(folds):
            page_out[
                i // pages_row,
                pl.ds((i % pages_row) * page_len, page_len),
                f * hd : (f + 1) * hd,
            ] = record[f * page_len : (f + 1) * page_len]
        return c

    pages_row = page_out.shape[1] // page_len
    lax.fori_loop(0, rows * pages_row, place_page, 0)
    context[0] = page_out[mine]
    for k in range(1, n_t):
        page_copy(k).start()

    def recall(r, c):
        alive = (lax.broadcasted_iota(jnp.int32, (tokens, 1), 0) < len_ref[r]).astype(F32)
        for h in range(heads):
            state = incoming[place[0, h * rows + r]]
            high, low = halves(coefs[r, h * tokens : (h + 1) * tokens, :])
            both = mm(jnp.concatenate([high, low], axis=0), state)
            seen = both[:tokens] + both[tokens:] + offsets[r, h * tokens : (h + 1) * tokens, :]
            recall_ref[r, :, h * hd : (h + 1) * hd] = (seen * alive).astype(BF16)
        return c

    lax.fori_loop(0, rows, recall, 0)

    for k in range(1, n_t):
        lift_copy(k).wait_recv()
        wuv_copy(k).wait_recv()
    for k in range(1, n_t):
        page_copy(k).wait_recv()

    every = heads * tokens
    scale = hd ** (-0.5)
    total_keys = context.shape[0] * context.shape[1]
    old_keys = n_t * context.shape[1]
    column = lax.broadcasted_iota(jnp.int32, (every, total_keys), 1) - old_keys
    token = lax.broadcasted_iota(jnp.int32, (every, total_keys), 0) % tokens
    row_alive = (lax.broadcasted_iota(jnp.int32, (tokens, 1), 0) < len_ref[mine]).astype(F32)

    def attend(k):
        keys = context[...].reshape(total_keys, latent)
        queries = lift_in[k].reshape(every, latent)
        scores = mm_nt(queries, keys) * scale
        scores = jnp.where(column <= token, scores, -1e30)
        top = jnp.max(scores, axis=-1, keepdims=True)
        e = jnp.exp(scores - top)
        total = jnp.sum(e, axis=-1, keepdims=True)
        mixed = mm(e.astype(BF16), keys)
        attended = (mixed / total).astype(BF16)
        for h in range(heads):
            out = mm(attended[h * tokens : (h + 1) * tokens], wuv_in[k, h]) * row_alive
            result_out[k, :, h * hd : (h + 1) * hd] = out.astype(BF16)

    def attend_away(k, c):
        attend(k)
        back_copy(k).start()
        return c

    lax.fori_loop(1, n_t, attend_away, 0)
    attend(0)
    mla_ref[mine] = result_out[0]

    for k in range(1, n_t):
        back_copy(k).wait_recv()
    for k in range(1, n_t):
        lift_copy(k).wait_send()
        wuv_copy(k).wait_send()
        page_copy(k).wait_send()
        back_copy(k).wait_send()
    for which in range(2):
        for k in range(1, side[which]):
            first_leg(which, k).wait_send()
        for j in range(1, side[1 - which]):
            column = incoming.at[pl.ds(spot(which, 1, 0, 0), side[which])]
            pltpu.make_async_copy(column, column, send_sem.at[which, 1, j]).wait()


def run_fused(
    sizes,
    tool_len,
    state_table,
    page_table,
    kda_pool,
    latent_pool,
    kda_q,
    kda_k,
    kda_v,
    kda_gate,
    kda_beta,
    mla_q,
    mla_new,
    w_uk,
    w_uv,
):
    heads, slots, hd, _ = kda_pool.shape
    _, pool_pages, page_len, latent = latent_pool.shape
    rows, tokens, _ = kda_q.shape
    pages_row = pool_pages // rows
    n_z, n_y, n_t = sizes
    n_dp = n_z * n_y
    lanes = state_table.shape[1]
    vmem = pl.BlockSpec(memory_space=pltpu.VMEM)
    smem = pl.BlockSpec(memory_space=pltpu.SMEM)
    out = jax.ShapeDtypeStruct(kda_q.shape, BF16)
    dma = pltpu.SemaphoreType.DMA
    return pl.pallas_call(
        functools.partial(fused, sizes),
        out_shape=(out, out),
        in_specs=[smem] + [pl.BlockSpec(memory_space=pl.ANY)] * 13,
        out_specs=(vmem, vmem),
        scratch_shapes=[
            pltpu.VMEM((heads * slots + pool_pages, hd, hd), BF16),
            pltpu.VMEM(kda_q.shape, BF16),
            pltpu.VMEM(kda_k.shape, BF16),
            pltpu.VMEM(kda_v.shape, BF16),
            pltpu.VMEM(kda_gate.shape, BF16),
            pltpu.VMEM(kda_beta.shape, BF16),
            pltpu.VMEM(mla_q.shape, BF16),
            pltpu.VMEM(mla_new.shape, BF16),
            pltpu.VMEM(w_uk.shape, BF16),
            pltpu.VMEM(w_uv.shape, BF16),
            pltpu.VMEM(state_table.shape, jnp.int32),
            pltpu.VMEM(page_table.shape[1:], jnp.int32),
            pltpu.VMEM((2, lanes), jnp.int32),
            pltpu.VMEM((1, LANES), jnp.int32),
            pltpu.SMEM((2, lanes), jnp.int32),
            pltpu.SMEM((1, LANES), jnp.int32),
            pltpu.VMEM((2, n_z, n_y, hd, hd), BF16),
            pltpu.VMEM((4 * n_dp, hd, hd), BF16),
            pltpu.VMEM((rows, heads, tokens, latent), BF16),
            pltpu.VMEM((n_t, heads, tokens, latent), BF16),
            pltpu.VMEM((n_t, heads, latent, hd), BF16),
            pltpu.VMEM((rows, pages_row * page_len, latent), BF16),
            pltpu.VMEM((n_t + 1, pages_row * page_len, latent), BF16),
            pltpu.VMEM((n_t, tokens, heads * hd), BF16),
            pltpu.VMEM((rows, heads * tokens, hd), F32),
            pltpu.VMEM((rows, heads * tokens, hd), F32),
            dma((2, 2, max(n_z, n_y))),
            dma((2, max(n_z, n_y))),
            dma((2, max(n_z, n_y))),
        ]
        + [dma((n_t,))] * 8
        + [dma((heads + latent // hd,)), dma((9,)), dma((4,))],
        compiler_params=pltpu.CompilerParams(
            collective_id=0, has_side_effects=True, vmem_limit_bytes=60 * 1024 * 1024
        ),
    )(
        tool_len,
        state_table,
        page_table,
        kda_pool,
        latent_pool,
        kda_q,
        kda_k,
        kda_v,
        kda_gate,
        kda_beta,
        mla_q,
        mla_new,
        w_uk,
        w_uv,
    )


def local(
    tool_len,
    state_table,
    page_table,
    kda_pool,
    latent_pool,
    kda_q,
    kda_k,
    kda_v,
    kda_gate,
    kda_beta,
    mla_q,
    mla_new,
    w_uk,
    w_uv,
):
    n_dp, n_t = lax.axis_size("dp"), lax.axis_size("tensor")
    return run_fused(
        (n_dp // SIDE_Y, SIDE_Y, n_t),
        tool_len,
        state_table.T,
        jnp.transpose(page_table, (1, 2, 0)),
        kda_pool,
        latent_pool,
        kda_q,
        kda_k,
        kda_v,
        kda_gate,
        kda_beta,
        mla_q,
        mla_new,
        w_uk,
        w_uv,
    )


def solution(mesh):
    in_specs = (
        P("dp"),
        P(),
        P(),
        P("tensor", "dp", None, None),
        P("tensor", "dp", None, None),
        P("dp", None, "tensor"),
        P("dp", None, "tensor"),
        P("dp", None, "tensor"),
        P("dp", None, "tensor"),
        P("dp", None, "tensor"),
        P("dp", None, "tensor"),
        P("dp", None, None),
        P("tensor", None, None),
        P("tensor", None, None),
    )
    out_specs = (P("dp", None, "tensor"), P("dp", None, "tensor"))
    return jax.shard_map(local, mesh=mesh, in_specs=in_specs, out_specs=out_specs, check_vma=False)
```

```python
import functools

import jax
import jax.numpy as jnp
from jax import lax
from jax.experimental import pallas as pl
from jax.experimental.pallas import tpu as pltpu
from jax.sharding import PartitionSpec as P

EPSILON = 1e-06
F32 = jnp.float32
BF16 = jnp.bfloat16
LANES = 128
SIDE_Y = 8


def mm(a, b):
    return lax.dot_general(a, b, (((1,), (0,)), ((), ())), preferred_element_type=F32)


def mm_nt(a, b):
    return lax.dot_general(a, b, (((1,), (1,)), ((), ())), preferred_element_type=F32)


def halves(values):
    high = values.astype(BF16)
    return high, (values - high.astype(F32)).astype(BF16)


def mm3(a, b, dot=mm):
    a_high, a_low = halves(a)
    b_high, b_low = halves(b)
    return dot(a_high, b_high) + (dot(a_high, b_low) + dot(a_low, b_high))


def unit_norm(values):
    return values / jnp.sqrt(jnp.sum(values * values, axis=-1, keepdims=True) + EPSILON)


def stack_heads(block, heads, width):
    return jnp.concatenate([block[:, h * width : (h + 1) * width] for h in range(heads)], axis=0)


def recall_coefficients(queries, keys, values, gates, betas, alive, tokens):
    rows = queries.shape[0]
    later = lax.broadcasted_iota(jnp.int32, (rows, rows), 0)
    sooner = lax.broadcasted_iota(jnp.int32, (rows, rows), 1)
    same = (later // tokens) == (sooner // tokens)
    reached = same & (sooner <= later)
    summed = mm(reached.astype(F32).astype(BF16), (gates.astype(F32) * alive).astype(BF16))
    grown = jnp.exp(summed)
    key_n = unit_norm(keys.astype(F32))
    query_up = unit_norm(queries.astype(F32)) * grown
    key_up = key_n * grown
    key_down = key_n * jnp.exp(-summed)
    mixing = mm3(key_up, key_down, mm_nt) * betas
    reach = jnp.where(reached, mm3(query_up, key_down, mm_nt), 0.0)
    inverse = (later == sooner).astype(F32)
    size = 1
    while size < tokens:
        pair = 2 * size
        corner = ((later // pair) == (sooner // pair)) & (later % pair >= size) & (sooner % pair < size)
        part = jnp.where(corner, mixing, 0.0)
        if size == 1:
            inverse = inverse - part
        else:
            inverse = inverse - mm3(mm3(inverse, part), inverse)
        size = pair
    spread = mm3(reach, inverse)
    coefficient = query_up - mm3(spread, betas * key_up)
    offset = mm3(spread, betas * values.astype(F32))
    return coefficient, offset


def routes(states, pages, me, side, rows, slots, pool_pages):
    n_z, n_y = side
    n_dp = n_z * n_y
    heads = states.shape[0]
    lanes = states.shape[1]
    kinds = heads + pages.shape[0]
    owners = jnp.concatenate([states // slots, pages // pool_pages], axis=0)
    head = lax.broadcasted_iota(jnp.int32, states.shape, 0)
    ids = jnp.concatenate(
        [head * slots + states % slots, heads * slots + pages % pool_pages], axis=0
    )
    here = owners == me
    first = jnp.min(jnp.where(here, ids, heads * slots + pool_pages - 1), axis=0, keepdims=True)
    second = jnp.max(jnp.where(here, ids, 0), axis=0, keepdims=True)
    span = 1
    while span < rows:
        first = jnp.minimum(first, pltpu.roll(first, lanes - span, 1))
        second = jnp.maximum(second, pltpu.roll(second, lanes - span, 1))
        span *= 2
    keys = owners * (heads * slots + pool_pages) + ids
    own = pltpu.roll(keys, (lanes - me * rows) % lanes, 1)[:, :LANES]
    place = lax.broadcasted_iota(jnp.int32, (1, LANES), 1)
    flat = jnp.zeros((1, LANES), jnp.int32)
    for kind in range(kinds):
        row = own[kind : kind + 1]
        if kind:
            row = pltpu.roll(row, kind * rows, 1)
        flat = jnp.where(place // rows == kind, row, flat)
    across = jnp.broadcast_to(flat, (LANES, LANES))
    down = jnp.transpose(across.astype(F32)).astype(jnp.int32)
    base = heads * slots + pool_pages
    valid = lax.broadcasted_iota(jnp.int32, (LANES, LANES), 0) < kinds * rows
    behind = valid & (down // base == across // base) & (down < across)
    late = jnp.max(behind.astype(F32), axis=0, keepdims=True).astype(jnp.int32)
    source = flat // base
    over_z = (me // n_y - source // n_y + n_z) % n_z
    over_y = (me % n_y - source % n_y + n_y) % n_y
    by_z = jnp.where(over_y == 0, 0, n_dp) + over_z * n_y + over_y
    by_y = jnp.where(over_z == 0, 0, n_dp) + over_y * n_z + over_z + 2 * n_dp
    return first, second, jnp.where(late == 0, by_z, by_y)


def fused(
    sizes,
    len_ref,
    state_table_ref,
    page_table_ref,
    states_ref,
    pages_ref,
    q_ref,
    k_ref,
    v_ref,
    gate_ref,
    beta_ref,
    mq_ref,
    new_ref,
    wuk_ref,
    wuv_ref,
    out_ref,
    records,
    q_buf,
    k_buf,
    v_buf,
    gate_buf,
    beta_buf,
    mq_buf,
    new_buf,
    wuk_buf,
    wuv_buf,
    state_slots,
    page_slots,
    picked_rows,
    place_row,
    picked,
    place,
    outgoing,
    incoming,
    lift_out,
    lift_in,
    wuv_in,
    page_out,
    context,
    result_out,
    coefs,
    offsets,
    scores,
    send_sem,
    first_sem,
    second_sem,
    swap_send_sem,
    swap_recv_sem,
    lift_send_sem,
    lift_recv_sem,
    wuv_send_sem,
    wuv_recv_sem,
    back_send_sem,
    back_recv_sem,
    record_sem,
    load_sem,
    table_sem,
):
    n_z, n_y, n_t = sizes
    n_dp = n_z * n_y
    side = (n_z, n_y)
    recall_ref, mla_ref = out_ref.at[0], out_ref.at[1]
    heads, slots, hd, _ = states_ref.shape
    page_len, latent = pages_ref.shape[2], pages_ref.shape[3]
    rows, tokens, _ = q_ref.shape
    folds = latent // hd
    me = lax.axis_index("dp")
    mine = lax.axis_index("tensor")
    at_z, at_y = me // n_y, me % n_y

    n_local = heads * slots
    record_loads = [
        pltpu.make_async_copy(
            states_ref.at[h], records.at[pl.ds(h * slots, slots)], record_sem.at[h]
        )
        for h in range(heads)
    ] + [
        pltpu.make_async_copy(
            pages_ref.at[0, :, :, f * hd : (f + 1) * hd],
            records.at[pl.ds(n_local, pages_ref.shape[1]), f * page_len : (f + 1) * page_len, :],
            record_sem.at[heads + f],
        )
        for f in range(folds)
    ]
    loads = [
        pltpu.make_async_copy(source, target, load_sem.at[i])
        for i, (source, target) in enumerate(
            (
                (mq_ref, mq_buf),
                (wuk_ref, wuk_buf),
                (wuv_ref, wuv_buf),
                (q_ref, q_buf),
                (k_ref, k_buf),
                (v_ref, v_buf),
                (gate_ref, gate_buf),
                (beta_ref, beta_buf),
                (new_ref, new_buf),
            )
        )
    ]
    table_loads = [
        pltpu.make_async_copy(state_table_ref, state_slots, table_sem.at[0]),
        pltpu.make_async_copy(page_table_ref.at[mine], page_slots, table_sem.at[1]),
    ]
    for load in table_loads + record_loads + loads:
        load.start()

    barrier = pltpu.get_barrier_semaphore()

    def greet_z(k, c):
        pl.semaphore_signal(barrier, inc=1, device_id={"dp": ((at_z + k) % n_z) * n_y + at_y})
        return c

    def greet_y(k, c):
        pl.semaphore_signal(barrier, inc=1, device_id={"dp": at_z * n_y + (at_y + k) % n_y})
        return c

    def greet_tensor(k, c):
        pl.semaphore_signal(barrier, inc=1, device_id={"tensor": (mine + k) % n_t})
        return c

    lax.fori_loop(1, n_z, greet_z, 0)
    lax.fori_loop(1, n_y, greet_y, 0)
    lax.fori_loop(1, n_t, greet_tensor, 0)

    for load in table_loads:
        load.wait()
    mine_slots = state_slots[0:heads, :]
    for t in range(1, n_t):
        mine_slots = jnp.where(mine == t, state_slots[t * heads : (t + 1) * heads, :], mine_slots)
    first, second, slot = routes(
        mine_slots,
        page_slots[...],
        me,
        (n_z, n_y),
        rows,
        slots,
        pages_ref.shape[1],
    )
    picked_rows[0:1, :] = first
    picked_rows[1:2, :] = second
    place_row[...] = slot
    scalars = [
        pltpu.make_async_copy(picked_rows, picked, table_sem.at[2]),
        pltpu.make_async_copy(place_row, place, table_sem.at[3]),
    ]
    for load in scalars:
        load.start()
    for load in scalars + record_loads:
        load.wait()

    def hop(which, leg, k):
        along_z = which == leg
        if along_z:
            return {"dp": ((at_z + k) % n_z) * n_y + at_y}
        return {"dp": at_z * n_y + (at_y + k) % n_y}

    def stage(which, k, j):
        over_z, over_y = (k, j) if which == 0 else (j, k)
        target = ((at_z + over_z) % n_z) * n_y + (at_y + over_y) % n_y
        return records[picked[which, target * rows]]

    def nearest(i, n):
        return (((i + 1) // 2) * (1 - 2 * ((i + 1) % 2)) + n) % n

    def spot(which, leg, k, j):
        return ((2 * which + leg) * side[which] + k) * side[1 - which] + j

    def first_leg(which, k):
        return pltpu.make_async_remote_copy(
            src_ref=outgoing.at[which, k],
            dst_ref=incoming.at[pl.ds(spot(which, 0, k, 0), side[1 - which])],
            send_sem=send_sem.at[which, 0, k],
            recv_sem=first_sem.at[which, k],
            device_id=hop(which, 0, k),
        )

    def second_leg(which, k, j, own):
        held = outgoing.at[which, k, j] if own else incoming.at[spot(which, 0, k, j)]
        return pltpu.make_async_remote_copy(
            src_ref=held,
            dst_ref=incoming.at[spot(which, 1, k, j)],
            send_sem=send_sem.at[which, 1, j],
            recv_sem=second_sem.at[which, j],
            device_id=hop(which, 1, j),
        )

    def forward(which, k, own):
        n = side[1 - which]

        def one(i, c):
            second_leg(which, k, nearest(i, n), own).start()
            return c

        lax.fori_loop(1, n, one, 0)

    for which in range(2):
        incoming[spot(which, 0, 0, 0)] = stage(which, 0, 0)

    pl.semaphore_wait(barrier, n_z + n_y + n_t - 3)

    def send_first(which, k):
        for j in range(side[1 - which]):
            outgoing[which, k, j] = stage(which, k, j)
        first_leg(which, k).start()

    for i in range(1, max(side)):
        for which in range(2):
            if i < side[which]:
                send_first(which, nearest(i, side[which]))
    for which in range(2):
        for j in range(1, side[1 - which]):
            outgoing[which, 0, j] = stage(which, 0, j)
        forward(which, 0, True)

    for load in loads:
        load.wait()

    for h in range(heads):
        queries = mq_buf[:, :, h * hd : (h + 1) * hd].reshape(rows * tokens, hd)
        lifted = mm(queries, wuk_buf[h]).astype(BF16)
        lift_out[:, h] = lifted.reshape(rows, tokens, latent)
    lift_in[0] = lift_out[mine]
    wuv_in[0] = wuv_buf[...]

    def lift_copy(k):
        peer = (mine + k) % n_t
        return pltpu.make_async_remote_copy(
            src_ref=lift_out.at[peer],
            dst_ref=lift_in.at[n_t - k],
            send_sem=lift_send_sem.at[k],
            recv_sem=lift_recv_sem.at[n_t - k],
            device_id={"tensor": peer},
        )

    def wuv_copy(k):
        peer = (mine + k) % n_t
        return pltpu.make_async_remote_copy(
            src_ref=wuv_buf,
            dst_ref=wuv_in.at[n_t - k],
            send_sem=wuv_send_sem.at[k],
            recv_sem=wuv_recv_sem.at[n_t - k],
            device_id={"tensor": peer},
        )

    def page_copy(k):
        peer = (mine + k) % n_t
        return pltpu.make_async_remote_copy(
            src_ref=page_out.at[peer],
            dst_ref=context.at[n_t - k],
            send_sem=swap_send_sem.at[k],
            recv_sem=swap_recv_sem.at[n_t - k],
            device_id={"tensor": peer},
        )

    def back_copy(k):
        peer = (mine + k) % n_t
        return pltpu.make_async_remote_copy(
            src_ref=result_out.at[k],
            dst_ref=mla_ref.at[mine],
            send_sem=back_send_sem.at[k],
            recv_sem=back_recv_sem.at[n_t - k],
            device_id={"tensor": peer},
        )

    for k in range(1, n_t):
        lift_copy(k).start()
    for k in range(1, n_t):
        wuv_copy(k).start()

    def make_coefficients(r, c):
        alive = (
            lax.broadcasted_iota(jnp.int32, (heads * tokens, 1), 0) % tokens < len_ref[r]
        ).astype(F32)
        raw = beta_buf[r].astype(F32)
        raw = jnp.concatenate([raw[h : h + 1] for h in range(heads)], axis=1)
        square = (heads * tokens, heads * tokens)
        diagonal = lax.broadcasted_iota(jnp.int32, square, 0) == lax.broadcasted_iota(
            jnp.int32, square, 1
        )
        raw = jnp.sum(jnp.where(diagonal, raw, 0.0), axis=1, keepdims=True)
        betas = alive / (1.0 + jnp.exp(-raw))
        coefficient, offset = recall_coefficients(
            stack_heads(q_buf[r], heads, hd),
            stack_heads(k_buf[r], heads, hd),
            stack_heads(v_buf[r], heads, hd),
            stack_heads(gate_buf[r], heads, hd),
            betas,
            alive,
            tokens,
        )
        coefs[r] = coefficient
        offsets[r] = offset
        return c

    def pass_on(i, c):
        for which in range(2):
            k = nearest(i, side[which])
            first_leg(which, k).wait_recv()
            forward(which, k, False)
        return c

    def work(i, c):
        make_coefficients(i - 1, c)
        return pass_on(i, c)

    assert n_z == n_y
    paired = min(rows, n_z - 1)
    lax.fori_loop(1, paired + 1, work, 0)
    lax.fori_loop(paired + 1, n_z, pass_on, 0)
    lax.fori_loop(paired, rows, make_coefficients, 0)

    fresh = new_buf[mine]
    context[n_t] = jnp.concatenate(
        [fresh, jnp.zeros((context.shape[1] - tokens, latent), BF16)], axis=0
    )

    for which in range(2):
        for j in range(1, side[1 - which]):
            column = incoming.at[pl.ds(spot(which, 1, 0, 0), side[which])]
            pltpu.make_async_copy(column, column, second_sem.at[which, j]).wait()

    n_states = heads * rows

    def place_page(i, c):
        record = incoming[place[0, n_states + (i % pages_row) * rows + i // pages_row]]
        for f in range(folds):
            page_out[
                i // pages_row,
                pl.ds((i % pages_row) * page_len, page_len),
                f * hd : (f + 1) * hd,
            ] = record[f * page_len : (f + 1) * page_len]
        return c

    pages_row = page_out.shape[1] // page_len
    lax.fori_loop(0, rows * pages_row, place_page, 0)
    context[0] = page_out[mine]
    for i in range(n_t - 1, 0, -1):
        page_copy(nearest(i, n_t)).start()

    def recall(r, c):
        alive = (lax.broadcasted_iota(jnp.int32, (tokens, 1), 0) < len_ref[r]).astype(F32)
        for h in range(heads):
            state = incoming[place[0, h * rows + r]]
            high, low = halves(coefs[r, h * tokens : (h + 1) * tokens, :])
            both = mm(jnp.concatenate([high, low], axis=0), state)
            seen = both[:tokens] + both[tokens:] + offsets[r, h * tokens : (h + 1) * tokens, :]
            recall_ref[r, :, h * hd : (h + 1) * hd] = (seen * alive).astype(BF16)
        return c

    lax.fori_loop(0, rows, recall, 0)

    for k in range(1, n_t):
        lift_copy(k).wait_recv()
        wuv_copy(k).wait_recv()

    every = heads * tokens
    queries = n_t * every
    width = context.shape[1]

    def score(i):
        scores[i] = mm_nt(lift_in[...].reshape(queries, latent), context[i])

    def score_arrived(i, c):
        k = nearest(i, n_t)
        page_copy(n_t - k).wait_recv()
        score(k)
        return c

    score(n_t)
    score(0)
    lax.fori_loop(1, n_t, score_arrived, 0)

    group = 2
    scale = hd ** (-0.5)
    seen_shape = (group * every, width)
    column = lax.broadcasted_iota(jnp.int32, seen_shape, 1)
    token = lax.broadcasted_iota(jnp.int32, seen_shape, 0) % tokens
    row_alive = (lax.broadcasted_iota(jnp.int32, (tokens, 1), 0) < len_ref[mine]).astype(F32)

    def attend(i):
        start = pl.multiple_of(i * group * every, group * every)
        parts = [scores[c, pl.ds(start, group * every), :] * scale for c in range(n_t + 1)]
        parts[n_t] = jnp.where(column <= token, parts[n_t], -1e30)
        top = functools.reduce(jnp.maximum, parts)
        top = jnp.max(top, axis=-1, keepdims=True)
        parts = [jnp.exp(part - top) for part in parts]
        total = jnp.sum(functools.reduce(jnp.add, parts), axis=-1, keepdims=True)
        weights = jnp.concatenate([part.astype(BF16) for part in parts], axis=1)
        mixed = mm(weights, context[...].reshape((n_t + 1) * width, latent))
        attended = (mixed / total).astype(BF16)
        for g in range(group):
            for h in range(heads):
                first = (g * heads + h) * tokens
                out = mm(attended[first : first + tokens], wuv_in[i * group + g, h]) * row_alive
                result_out[i * group + g, :, h * hd : (h + 1) * hd] = out.astype(BF16)

    def attend_away(i, c):
        attend(i)
        for g in range(group):
            back_copy(i * group + g).start()
        return c

    lax.fori_loop(1, n_t // group, attend_away, 0)
    attend(0)
    for g in range(1, group):
        back_copy(g).start()
    mla_ref[mine] = result_out[0]

    for k in range(1, n_t):
        back_copy(k).wait_recv()
    for k in range(1, n_t):
        lift_copy(k).wait_send()
        wuv_copy(k).wait_send()
        page_copy(k).wait_send()
        back_copy(k).wait_send()
    for which in range(2):
        for k in range(1, side[which]):
            first_leg(which, k).wait_send()
        for j in range(1, side[1 - which]):
            column = incoming.at[pl.ds(spot(which, 1, 0, 0), side[which])]
            pltpu.make_async_copy(column, column, send_sem.at[which, 1, j]).wait()


def run_fused(
    sizes,
    tool_len,
    state_table,
    page_table,
    kda_pool,
    latent_pool,
    kda_q,
    kda_k,
    kda_v,
    kda_gate,
    kda_beta,
    mla_q,
    mla_new,
    w_uk,
    w_uv,
):
    heads, slots, hd, _ = kda_pool.shape
    _, pool_pages, page_len, latent = latent_pool.shape
    rows, tokens, _ = kda_q.shape
    pages_row = pool_pages // rows
    n_z, n_y, n_t = sizes
    n_dp = n_z * n_y
    lanes = state_table.shape[1]
    vmem = pl.BlockSpec(memory_space=pltpu.VMEM)
    smem = pl.BlockSpec(memory_space=pltpu.SMEM)
    out = jax.ShapeDtypeStruct((2,) + kda_q.shape, BF16)
    dma = pltpu.SemaphoreType.DMA
    both = pl.pallas_call(
        functools.partial(fused, sizes),
        out_shape=out,
        in_specs=[smem] + [pl.BlockSpec(memory_space=pl.ANY)] * 13,
        out_specs=vmem,
        scratch_shapes=[
            pltpu.VMEM((heads * slots + pool_pages, hd, hd), BF16),
            pltpu.VMEM(kda_q.shape, BF16),
            pltpu.VMEM(kda_k.shape, BF16),
            pltpu.VMEM(kda_v.shape, BF16),
            pltpu.VMEM(kda_gate.shape, BF16),
            pltpu.VMEM(kda_beta.shape, BF16),
            pltpu.VMEM(mla_q.shape, BF16),
            pltpu.VMEM(mla_new.shape, BF16),
            pltpu.VMEM(w_uk.shape, BF16),
            pltpu.VMEM(w_uv.shape, BF16),
            pltpu.VMEM(state_table.shape, jnp.int32),
            pltpu.VMEM(page_table.shape[1:], jnp.int32),
            pltpu.VMEM((2, lanes), jnp.int32),
            pltpu.VMEM((1, LANES), jnp.int32),
            pltpu.SMEM((2, lanes), jnp.int32),
            pltpu.SMEM((1, LANES), jnp.int32),
            pltpu.VMEM((2, n_z, n_y, hd, hd), BF16),
            pltpu.VMEM((4 * n_dp, hd, hd), BF16),
            pltpu.VMEM((rows, heads, tokens, latent), BF16),
            pltpu.VMEM((n_t, heads, tokens, latent), BF16),
            pltpu.VMEM((n_t, heads, latent, hd), BF16),
            pltpu.VMEM((rows, pages_row * page_len, latent), BF16),
            pltpu.VMEM((n_t + 1, pages_row * page_len, latent), BF16),
            pltpu.VMEM((n_t, tokens, heads * hd), BF16),
            pltpu.VMEM((rows, heads * tokens, hd), F32),
            pltpu.VMEM((rows, heads * tokens, hd), F32),
            pltpu.VMEM((n_t + 1, n_t * heads * tokens, pages_row * page_len), F32),
            dma((2, 2, max(n_z, n_y))),
            dma((2, max(n_z, n_y))),
            dma((2, max(n_z, n_y))),
        ]
        + [dma((n_t,))] * 8
        + [dma((heads + latent // hd,)), dma((9,)), dma((4,))],
        compiler_params=pltpu.CompilerParams(
            collective_id=0, has_side_effects=True, vmem_limit_bytes=60 * 1024 * 1024
        ),
    )(
        tool_len,
        state_table,
        page_table,
        kda_pool,
        latent_pool,
        kda_q,
        kda_k,
        kda_v,
        kda_gate,
        kda_beta,
        mla_q,
        mla_new,
        w_uk,
        w_uv,
    )
    return both[0], both[1]


def local(
    tool_len,
    state_table,
    page_table,
    kda_pool,
    latent_pool,
    kda_q,
    kda_k,
    kda_v,
    kda_gate,
    kda_beta,
    mla_q,
    mla_new,
    w_uk,
    w_uv,
):
    n_dp, n_t = lax.axis_size("dp"), lax.axis_size("tensor")
    return run_fused(
        (n_dp // SIDE_Y, SIDE_Y, n_t),
        tool_len,
        state_table.T,
        jnp.transpose(page_table, (1, 2, 0)),
        kda_pool,
        latent_pool,
        kda_q,
        kda_k,
        kda_v,
        kda_gate,
        jnp.transpose(kda_beta, (0, 2, 1)),
        mla_q,
        mla_new,
        w_uk,
        w_uv,
    )


def solution(mesh):
    in_specs = (
        P("dp"),
        P(),
        P(),
        P("tensor", "dp", None, None),
        P("tensor", "dp", None, None),
        P("dp", None, "tensor"),
        P("dp", None, "tensor"),
        P("dp", None, "tensor"),
        P("dp", None, "tensor"),
        P("dp", None, "tensor"),
        P("dp", None, "tensor"),
        P("dp", None, None),
        P("tensor", None, None),
        P("tensor", None, None),
    )
    out_specs = (P("dp", None, "tensor"), P("dp", None, "tensor"))
    return jax.shard_map(local, mesh=mesh, in_specs=in_specs, out_specs=out_specs, check_vma=False)
```

```python
import functools

import jax
import jax.numpy as jnp
from jax import lax
from jax.experimental import pallas as pl
from jax.experimental.pallas import tpu as pltpu
from jax.sharding import PartitionSpec as P

EPSILON = 1e-06
F32 = jnp.float32
BF16 = jnp.bfloat16
LANES = 128
SIDE_Y = 8


def mm(a, b):
    return lax.dot_general(a, b, (((1,), (0,)), ((), ())), preferred_element_type=F32)


def mm_nt(a, b):
    return lax.dot_general(a, b, (((1,), (1,)), ((), ())), preferred_element_type=F32)


def halves(values):
    high = values.astype(BF16)
    return high, (values - high.astype(F32)).astype(BF16)


def mm3(a, b, dot=mm):
    a_high, a_low = halves(a)
    b_high, b_low = halves(b)
    return dot(a_high, b_high) + (dot(a_high, b_low) + dot(a_low, b_high))


def unit_norm(values):
    return values / jnp.sqrt(jnp.sum(values * values, axis=-1, keepdims=True) + EPSILON)


def stack_heads(block, heads, width):
    return jnp.concatenate([block[:, h * width : (h + 1) * width] for h in range(heads)], axis=0)


def recall_coefficients(queries, keys, values, gates, betas, alive, tokens):
    rows = queries.shape[0]
    later = lax.broadcasted_iota(jnp.int32, (rows, rows), 0)
    sooner = lax.broadcasted_iota(jnp.int32, (rows, rows), 1)
    same = (later // tokens) == (sooner // tokens)
    reached = same & (sooner <= later)
    summed = mm(reached.astype(F32).astype(BF16), (gates.astype(F32) * alive).astype(BF16))
    grown = jnp.exp(summed)
    key_n = unit_norm(keys.astype(F32))
    query_up = unit_norm(queries.astype(F32)) * grown
    key_up = key_n * grown
    key_down = key_n * jnp.exp(-summed)
    mixing = mm3(key_up, key_down, mm_nt) * betas
    reach = jnp.where(reached, mm3(query_up, key_down, mm_nt), 0.0)
    inverse = (later == sooner).astype(F32)
    size = 1
    while size < tokens:
        pair = 2 * size
        corner = ((later // pair) == (sooner // pair)) & (later % pair >= size) & (sooner % pair < size)
        part = jnp.where(corner, mixing, 0.0)
        if size == 1:
            inverse = inverse - part
        else:
            inverse = inverse - mm3(mm3(inverse, part), inverse)
        size = pair
    spread = mm3(reach, inverse)
    coefficient = query_up - mm3(spread, betas * key_up)
    offset = mm3(spread, betas * values.astype(F32))
    return coefficient, offset


def routes(states, pages, me, side, rows, slots, pool_pages):
    n_z, n_y = side
    n_dp = n_z * n_y
    heads = states.shape[0]
    lanes = states.shape[1]
    kinds = heads + pages.shape[0]
    owners = jnp.concatenate([states // slots, pages // pool_pages], axis=0)
    head = lax.broadcasted_iota(jnp.int32, states.shape, 0)
    ids = jnp.concatenate(
        [head * slots + states % slots, heads * slots + pages % pool_pages], axis=0
    )
    here = owners == me
    first = jnp.min(jnp.where(here, ids, heads * slots + pool_pages - 1), axis=0, keepdims=True)
    second = jnp.max(jnp.where(here, ids, 0), axis=0, keepdims=True)
    span = 1
    while span < rows:
        first = jnp.minimum(first, pltpu.roll(first, lanes - span, 1))
        second = jnp.maximum(second, pltpu.roll(second, lanes - span, 1))
        span *= 2
    keys = owners * (heads * slots + pool_pages) + ids
    own = pltpu.roll(keys, (lanes - me * rows) % lanes, 1)[:, :LANES]
    place = lax.broadcasted_iota(jnp.int32, (1, LANES), 1)
    flat = jnp.zeros((1, LANES), jnp.int32)
    for kind in range(kinds):
        row = own[kind : kind + 1]
        if kind:
            row = pltpu.roll(row, kind * rows, 1)
        flat = jnp.where(place // rows == kind, row, flat)
    across = jnp.broadcast_to(flat, (LANES, LANES))
    down = jnp.transpose(across.astype(F32)).astype(jnp.int32)
    base = heads * slots + pool_pages
    valid = lax.broadcasted_iota(jnp.int32, (LANES, LANES), 0) < kinds * rows
    behind = valid & (down // base == across // base) & (down < across)
    late = jnp.max(behind.astype(F32), axis=0, keepdims=True).astype(jnp.int32)
    source = flat // base
    over_z = (me // n_y - source // n_y + n_z) % n_z
    over_y = (me % n_y - source % n_y + n_y) % n_y
    by_z = jnp.where(over_y == 0, 0, n_dp) + over_z * n_y + over_y
    by_y = jnp.where(over_z == 0, 0, n_dp) + over_y * n_z + over_z + 2 * n_dp
    return first, second, jnp.where(late == 0, by_z, by_y)


def fused(
    sizes,
    len_ref,
    state_table_ref,
    page_table_ref,
    states_ref,
    pages_ref,
    q_ref,
    k_ref,
    v_ref,
    gate_ref,
    beta_ref,
    mq_ref,
    new_ref,
    wuk_ref,
    wuv_ref,
    out_ref,
    records,
    q_buf,
    k_buf,
    v_buf,
    gate_buf,
    beta_buf,
    mq_buf,
    new_buf,
    wuk_buf,
    wuv_buf,
    state_slots,
    page_slots,
    picked_rows,
    place_row,
    picked,
    place,
    outgoing,
    incoming,
    lift_out,
    lift_in,
    wuv_in,
    page_out,
    context,
    result_out,
    coefs,
    offsets,
    tops,
    sums,
    mixes,
    send_sem,
    first_sem,
    second_sem,
    swap_send_sem,
    swap_recv_sem,
    lift_send_sem,
    lift_recv_sem,
    wuv_send_sem,
    wuv_recv_sem,
    back_send_sem,
    back_recv_sem,
    record_sem,
    load_sem,
    table_sem,
):
    n_z, n_y, n_t = sizes
    n_dp = n_z * n_y
    side = (n_z, n_y)
    recall_ref, mla_ref = out_ref.at[0], out_ref.at[1]
    heads, slots, hd, _ = states_ref.shape
    page_len, latent = pages_ref.shape[2], pages_ref.shape[3]
    rows, tokens, _ = q_ref.shape
    folds = latent // hd
    me = lax.axis_index("dp")
    mine = lax.axis_index("tensor")
    at_z, at_y = me // n_y, me % n_y

    n_local = heads * slots
    record_loads = [
        pltpu.make_async_copy(
            states_ref.at[h], records.at[pl.ds(h * slots, slots)], record_sem.at[h]
        )
        for h in range(heads)
    ] + [
        pltpu.make_async_copy(
            pages_ref.at[0, :, :, f * hd : (f + 1) * hd],
            records.at[pl.ds(n_local, pages_ref.shape[1]), f * page_len : (f + 1) * page_len, :],
            record_sem.at[heads + f],
        )
        for f in range(folds)
    ]
    loads = [
        pltpu.make_async_copy(source, target, load_sem.at[i])
        for i, (source, target) in enumerate(
            (
                (mq_ref, mq_buf),
                (wuk_ref, wuk_buf),
                (wuv_ref, wuv_buf),
                (q_ref, q_buf),
                (k_ref, k_buf),
                (v_ref, v_buf),
                (gate_ref, gate_buf),
                (beta_ref, beta_buf),
                (new_ref, new_buf),
            )
        )
    ]
    table_loads = [
        pltpu.make_async_copy(state_table_ref, state_slots, table_sem.at[0]),
        pltpu.make_async_copy(page_table_ref.at[mine], page_slots, table_sem.at[1]),
    ]
    for load in table_loads + record_loads + loads:
        load.start()

    barrier = pltpu.get_barrier_semaphore()

    def greet_z(k, c):
        pl.semaphore_signal(barrier, inc=1, device_id={"dp": ((at_z + k) % n_z) * n_y + at_y})
        return c

    def greet_y(k, c):
        pl.semaphore_signal(barrier, inc=1, device_id={"dp": at_z * n_y + (at_y + k) % n_y})
        return c

    def greet_tensor(k, c):
        pl.semaphore_signal(barrier, inc=1, device_id={"tensor": (mine + k) % n_t})
        return c

    lax.fori_loop(1, n_z, greet_z, 0)
    lax.fori_loop(1, n_y, greet_y, 0)
    lax.fori_loop(1, n_t, greet_tensor, 0)

    for load in table_loads:
        load.wait()
    mine_slots = state_slots[0:heads, :]
    for t in range(1, n_t):
        mine_slots = jnp.where(mine == t, state_slots[t * heads : (t + 1) * heads, :], mine_slots)
    first, second, slot = routes(
        mine_slots,
        page_slots[...],
        me,
        (n_z, n_y),
        rows,
        slots,
        pages_ref.shape[1],
    )
    picked_rows[0:1, :] = first
    picked_rows[1:2, :] = second
    place_row[...] = slot
    scalars = [
        pltpu.make_async_copy(picked_rows, picked, table_sem.at[2]),
        pltpu.make_async_copy(place_row, place, table_sem.at[3]),
    ]
    for load in scalars:
        load.start()
    for load in scalars + record_loads:
        load.wait()

    def hop(which, leg, k):
        along_z = which == leg
        if along_z:
            return {"dp": ((at_z + k) % n_z) * n_y + at_y}
        return {"dp": at_z * n_y + (at_y + k) % n_y}

    def stage(which, k, j):
        over_z, over_y = (k, j) if which == 0 else (j, k)
        target = ((at_z + over_z) % n_z) * n_y + (at_y + over_y) % n_y
        return records[picked[which, target * rows]]

    def nearest(i, n):
        return (((i + 1) // 2) * (1 - 2 * ((i + 1) % 2)) + n) % n

    def spot(which, leg, k, j):
        return ((2 * which + leg) * side[which] + k) * side[1 - which] + j

    def first_leg(which, k):
        return pltpu.make_async_remote_copy(
            src_ref=outgoing.at[which, k],
            dst_ref=incoming.at[pl.ds(spot(which, 0, k, 0), side[1 - which])],
            send_sem=send_sem.at[which, 0, k],
            recv_sem=first_sem.at[which, k],
            device_id=hop(which, 0, k),
        )

    def second_leg(which, k, j, own):
        held = outgoing.at[which, k, j] if own else incoming.at[spot(which, 0, k, j)]
        return pltpu.make_async_remote_copy(
            src_ref=held,
            dst_ref=incoming.at[spot(which, 1, k, j)],
            send_sem=send_sem.at[which, 1, j],
            recv_sem=second_sem.at[which, j],
            device_id=hop(which, 1, j),
        )

    def forward(which, k, own):
        n = side[1 - which]

        def one(i, c):
            second_leg(which, k, nearest(i, n), own).start()
            return c

        lax.fori_loop(1, n, one, 0)

    for which in range(2):
        incoming[spot(which, 0, 0, 0)] = stage(which, 0, 0)

    pl.semaphore_wait(barrier, n_z + n_y + n_t - 3)

    def send_first(which, k):
        for j in range(side[1 - which]):
            outgoing[which, k, j] = stage(which, k, j)
        first_leg(which, k).start()

    for i in range(1, max(side)):
        for which in range(2):
            if i < side[which]:
                send_first(which, nearest(i, side[which]))
    for which in range(2):
        for j in range(1, side[1 - which]):
            outgoing[which, 0, j] = stage(which, 0, j)
        forward(which, 0, True)

    for load in loads:
        load.wait()

    for h in range(heads):
        queries = mq_buf[:, :, h * hd : (h + 1) * hd].reshape(rows * tokens, hd)
        lifted = mm(queries, wuk_buf[h]).astype(BF16)
        lift_out[:, h] = lifted.reshape(rows, tokens, latent)
    lift_in[0] = lift_out[mine]
    wuv_in[0] = wuv_buf[...]

    def lift_copy(k):
        peer = (mine + k) % n_t
        return pltpu.make_async_remote_copy(
            src_ref=lift_out.at[peer],
            dst_ref=lift_in.at[n_t - k],
            send_sem=lift_send_sem.at[k],
            recv_sem=lift_recv_sem.at[n_t - k],
            device_id={"tensor": peer},
        )

    def wuv_copy(k):
        peer = (mine + k) % n_t
        return pltpu.make_async_remote_copy(
            src_ref=wuv_buf,
            dst_ref=wuv_in.at[n_t - k],
            send_sem=wuv_send_sem.at[k],
            recv_sem=wuv_recv_sem.at[n_t - k],
            device_id={"tensor": peer},
        )

    def page_copy(k):
        peer = (mine + k) % n_t
        return pltpu.make_async_remote_copy(
            src_ref=page_out.at[peer],
            dst_ref=context.at[n_t - k],
            send_sem=swap_send_sem.at[k],
            recv_sem=swap_recv_sem.at[n_t - k],
            device_id={"tensor": peer},
        )

    def back_copy(k):
        peer = (mine + k) % n_t
        return pltpu.make_async_remote_copy(
            src_ref=result_out.at[k],
            dst_ref=mla_ref.at[mine],
            send_sem=back_send_sem.at[k],
            recv_sem=back_recv_sem.at[n_t - k],
            device_id={"tensor": peer},
        )

    for k in range(1, n_t):
        lift_copy(k).start()
    for k in range(1, n_t):
        wuv_copy(k).start()

    def make_coefficients(r, c):
        alive = (
            lax.broadcasted_iota(jnp.int32, (heads * tokens, 1), 0) % tokens < len_ref[r]
        ).astype(F32)
        raw = beta_buf[r].astype(F32)
        raw = jnp.concatenate([raw[h : h + 1] for h in range(heads)], axis=1)
        square = (heads * tokens, heads * tokens)
        diagonal = lax.broadcasted_iota(jnp.int32, square, 0) == lax.broadcasted_iota(
            jnp.int32, square, 1
        )
        raw = jnp.sum(jnp.where(diagonal, raw, 0.0), axis=1, keepdims=True)
        betas = alive / (1.0 + jnp.exp(-raw))
        coefficient, offset = recall_coefficients(
            stack_heads(q_buf[r], heads, hd),
            stack_heads(k_buf[r], heads, hd),
            stack_heads(v_buf[r], heads, hd),
            stack_heads(gate_buf[r], heads, hd),
            betas,
            alive,
            tokens,
        )
        coefs[r] = coefficient
        offsets[r] = offset
        return c

    def pass_on(i, c):
        for which in range(2):
            k = nearest(i, side[which])
            first_leg(which, k).wait_recv()
            forward(which, k, False)
        return c

    def work(i, c):
        make_coefficients(i - 1, c)
        return pass_on(i, c)

    assert n_z == n_y
    paired = min(rows, n_z - 1)
    lax.fori_loop(1, paired + 1, work, 0)
    lax.fori_loop(paired + 1, n_z, pass_on, 0)
    lax.fori_loop(paired, rows, make_coefficients, 0)

    fresh = new_buf[mine]
    context[n_t] = jnp.concatenate(
        [fresh, jnp.zeros((context.shape[1] - tokens, latent), BF16)], axis=0
    )

    for which in range(2):
        for j in range(1, side[1 - which]):
            column = incoming.at[pl.ds(spot(which, 1, 0, 0), side[which])]
            pltpu.make_async_copy(column, column, second_sem.at[which, j]).wait()

    n_states = heads * rows

    def place_page(i, c):
        record = incoming[place[0, n_states + (i % pages_row) * rows + i // pages_row]]
        for f in range(folds):
            page_out[
                i // pages_row,
                pl.ds((i % pages_row) * page_len, page_len),
                f * hd : (f + 1) * hd,
            ] = record[f * page_len : (f + 1) * page_len]
        return c

    pages_row = page_out.shape[1] // page_len
    lax.fori_loop(0, rows * pages_row, place_page, 0)
    context[0] = page_out[mine]
    odd = mine % 2
    twin = 1 + (n_t - 2) * odd
    far = n_t // 4
    near_chips = [p for p in range(1, n_t // 2) if p != far]

    def cores(p):
        return (2 * p - odd, 2 * p + 1 - odd)

    page_copy(twin).start()
    for p in near_chips + [far]:
        for k in cores(p):
            page_copy(k).start()

    def recall(r, c):
        alive = (lax.broadcasted_iota(jnp.int32, (tokens, 1), 0) < len_ref[r]).astype(F32)
        for h in range(heads):
            state = incoming[place[0, h * rows + r]]
            high, low = halves(coefs[r, h * tokens : (h + 1) * tokens, :])
            both = mm(jnp.concatenate([high, low], axis=0), state)
            seen = both[:tokens] + both[tokens:] + offsets[r, h * tokens : (h + 1) * tokens, :]
            recall_ref[r, :, h * hd : (h + 1) * hd] = (seen * alive).astype(BF16)
        return c

    lax.fori_loop(0, rows, recall, 0)

    for k in range(1, n_t):
        lift_copy(k).wait_recv()
        wuv_copy(k).wait_recv()

    every = heads * tokens
    width = context.shape[1]
    group = 2
    size = group * every
    scale = hd ** (-0.5)
    column = lax.broadcasted_iota(jnp.int32, (size, width), 1)
    token = lax.broadcasted_iota(jnp.int32, (size, width), 0) % tokens
    row_alive = (lax.broadcasted_iota(jnp.int32, (tokens, 1), 0) < len_ref[mine]).astype(F32)

    def asked(i):
        return lift_in[i * group : (i + 1) * group].reshape(size, latent)

    def chip(p):
        return context[pl.ds(2 * p - odd, 2)].reshape(2 * width, latent)

    def arrive(k):
        page_copy(n_t - k).wait_recv()

    arrive(twin)
    for p in near_chips:
        for k in cores(p):
            arrive(k)
    for i in range(n_t // group):
        span = slice(i * size, (i + 1) * size)
        keys = [context[n_t], context[0], context[twin]] + [chip(p) for p in near_chips]
        parts = [mm_nt(asked(i), key) * scale for key in keys]
        parts[0] = jnp.where(column <= token, parts[0], -1e30)
        top = functools.reduce(
            jnp.maximum, [jnp.max(part, axis=-1, keepdims=True) for part in parts]
        )
        parts = [jnp.exp(part - top) for part in parts]
        tops[span] = top
        sums[span] = functools.reduce(
            jnp.add, [jnp.sum(part, axis=-1, keepdims=True) for part in parts]
        )
        mixes[span] = functools.reduce(
            jnp.add, [mm(part.astype(BF16), key) for part, key in zip(parts, keys)]
        )

    for k in cores(far):
        arrive(k)
    for i in [*range(1, n_t // group), 0]:
        span = slice(i * size, (i + 1) * size)
        key = chip(far)
        part = mm_nt(asked(i), key) * scale
        top = jnp.maximum(tops[span], jnp.max(part, axis=-1, keepdims=True))
        part = jnp.exp(part - top)
        fade = jnp.exp(tops[span] - top)
        share = 1.0 / (fade * sums[span] + jnp.sum(part, axis=-1, keepdims=True))
        attended = (fade * share * mixes[span] + share * mm(part.astype(BF16), key)).astype(BF16)
        for g in range(group):
            k = i * group + g
            for h in range(heads):
                first = (g * heads + h) * tokens
                out = mm(attended[first : first + tokens], wuv_in[k, h]) * row_alive
                result_out[k, :, h * hd : (h + 1) * hd] = out.astype(BF16)
            if k:
                back_copy(k).start()
    mla_ref[mine] = result_out[0]

    for k in range(1, n_t):
        back_copy(k).wait_recv()
    for k in range(1, n_t):
        lift_copy(k).wait_send()
        wuv_copy(k).wait_send()
        page_copy(k).wait_send()
        back_copy(k).wait_send()
    for which in range(2):
        for k in range(1, side[which]):
            first_leg(which, k).wait_send()
        for j in range(1, side[1 - which]):
            column = incoming.at[pl.ds(spot(which, 1, 0, 0), side[which])]
            pltpu.make_async_copy(column, column, send_sem.at[which, 1, j]).wait()


def run_fused(
    sizes,
    tool_len,
    state_table,
    page_table,
    kda_pool,
    latent_pool,
    kda_q,
    kda_k,
    kda_v,
    kda_gate,
    kda_beta,
    mla_q,
    mla_new,
    w_uk,
    w_uv,
):
    heads, slots, hd, _ = kda_pool.shape
    _, pool_pages, page_len, latent = latent_pool.shape
    rows, tokens, _ = kda_q.shape
    pages_row = pool_pages // rows
    n_z, n_y, n_t = sizes
    n_dp = n_z * n_y
    lanes = state_table.shape[1]
    vmem = pl.BlockSpec(memory_space=pltpu.VMEM)
    smem = pl.BlockSpec(memory_space=pltpu.SMEM)
    out = jax.ShapeDtypeStruct((2,) + kda_q.shape, BF16)
    dma = pltpu.SemaphoreType.DMA
    both = pl.pallas_call(
        functools.partial(fused, sizes),
        out_shape=out,
        in_specs=[smem] + [pl.BlockSpec(memory_space=pl.ANY)] * 13,
        out_specs=vmem,
        scratch_shapes=[
            pltpu.VMEM((heads * slots + pool_pages, hd, hd), BF16),
            pltpu.VMEM(kda_q.shape, BF16),
            pltpu.VMEM(kda_k.shape, BF16),
            pltpu.VMEM(kda_v.shape, BF16),
            pltpu.VMEM(kda_gate.shape, BF16),
            pltpu.VMEM(kda_beta.shape, BF16),
            pltpu.VMEM(mla_q.shape, BF16),
            pltpu.VMEM(mla_new.shape, BF16),
            pltpu.VMEM(w_uk.shape, BF16),
            pltpu.VMEM(w_uv.shape, BF16),
            pltpu.VMEM(state_table.shape, jnp.int32),
            pltpu.VMEM(page_table.shape[1:], jnp.int32),
            pltpu.VMEM((2, lanes), jnp.int32),
            pltpu.VMEM((1, LANES), jnp.int32),
            pltpu.SMEM((2, lanes), jnp.int32),
            pltpu.SMEM((1, LANES), jnp.int32),
            pltpu.VMEM((2, n_z, n_y, hd, hd), BF16),
            pltpu.VMEM((4 * n_dp, hd, hd), BF16),
            pltpu.VMEM((rows, heads, tokens, latent), BF16),
            pltpu.VMEM((n_t, heads, tokens, latent), BF16),
            pltpu.VMEM((n_t, heads, latent, hd), BF16),
            pltpu.VMEM((rows, pages_row * page_len, latent), BF16),
            pltpu.VMEM((n_t + 1, pages_row * page_len, latent), BF16),
            pltpu.VMEM((n_t, tokens, heads * hd), BF16),
            pltpu.VMEM((rows, heads * tokens, hd), F32),
            pltpu.VMEM((rows, heads * tokens, hd), F32),
            pltpu.VMEM((n_t * heads * tokens, 1), F32),
            pltpu.VMEM((n_t * heads * tokens, 1), F32),
            pltpu.VMEM((n_t * heads * tokens, latent), F32),
            dma((2, 2, max(n_z, n_y))),
            dma((2, max(n_z, n_y))),
            dma((2, max(n_z, n_y))),
        ]
        + [dma((n_t,))] * 8
        + [dma((heads + latent // hd,)), dma((9,)), dma((4,))],
        compiler_params=pltpu.CompilerParams(
            collective_id=0, has_side_effects=True, vmem_limit_bytes=60 * 1024 * 1024
        ),
    )(
        tool_len,
        state_table,
        page_table,
        kda_pool,
        latent_pool,
        kda_q,
        kda_k,
        kda_v,
        kda_gate,
        kda_beta,
        mla_q,
        mla_new,
        w_uk,
        w_uv,
    )
    return both[0], both[1]


def local(
    tool_len,
    state_table,
    page_table,
    kda_pool,
    latent_pool,
    kda_q,
    kda_k,
    kda_v,
    kda_gate,
    kda_beta,
    mla_q,
    mla_new,
    w_uk,
    w_uv,
):
    n_dp, n_t = lax.axis_size("dp"), lax.axis_size("tensor")
    return run_fused(
        (n_dp // SIDE_Y, SIDE_Y, n_t),
        tool_len,
        state_table.T,
        jnp.transpose(page_table, (1, 2, 0)),
        kda_pool,
        latent_pool,
        kda_q,
        kda_k,
        kda_v,
        kda_gate,
        jnp.transpose(kda_beta, (0, 2, 1)),
        mla_q,
        mla_new,
        w_uk,
        w_uv,
    )


def solution(mesh):
    in_specs = (
        P("dp"),
        P(),
        P(),
        P("tensor", "dp", None, None),
        P("tensor", "dp", None, None),
        P("dp", None, "tensor"),
        P("dp", None, "tensor"),
        P("dp", None, "tensor"),
        P("dp", None, "tensor"),
        P("dp", None, "tensor"),
        P("dp", None, "tensor"),
        P("dp", None, None),
        P("tensor", None, None),
        P("tensor", None, None),
    )
    out_specs = (P("dp", None, "tensor"), P("dp", None, "tensor"))
    return jax.shard_map(local, mesh=mesh, in_specs=in_specs, out_specs=out_specs, check_vma=False)
```

```python
import functools

import jax
import jax.numpy as jnp
from jax import lax
from jax.experimental import pallas as pl
from jax.experimental.pallas import tpu as pltpu
from jax.sharding import PartitionSpec as P

EPSILON = 1e-06
F32 = jnp.float32
BF16 = jnp.bfloat16
LANES = 128
SIDE_Y = 8


def mm(a, b):
    return lax.dot_general(a, b, (((1,), (0,)), ((), ())), preferred_element_type=F32)


def mm_nt(a, b):
    return lax.dot_general(a, b, (((1,), (1,)), ((), ())), preferred_element_type=F32)


def halves(values):
    high = values.astype(BF16)
    return high, (values - high.astype(F32)).astype(BF16)


def mm3(a, b, dot=mm):
    a_high, a_low = halves(a)
    b_high, b_low = halves(b)
    return dot(a_high, b_high) + (dot(a_high, b_low) + dot(a_low, b_high))


def unit_norm(values):
    return values / jnp.sqrt(jnp.sum(values * values, axis=-1, keepdims=True) + EPSILON)


def stack_heads(block, heads, width):
    return jnp.concatenate([block[:, h * width : (h + 1) * width] for h in range(heads)], axis=0)


def recall_coefficients(queries, keys, values, gates, betas, alive, tokens):
    rows = queries.shape[0]
    later = lax.broadcasted_iota(jnp.int32, (rows, rows), 0)
    sooner = lax.broadcasted_iota(jnp.int32, (rows, rows), 1)
    same = (later // tokens) == (sooner // tokens)
    reached = same & (sooner <= later)
    summed = mm(reached.astype(F32).astype(BF16), (gates.astype(F32) * alive).astype(BF16))
    grown = jnp.exp(summed)
    key_n = unit_norm(keys.astype(F32))
    query_up = unit_norm(queries.astype(F32)) * grown
    key_up = key_n * grown
    key_down = key_n * jnp.exp(-summed)
    mixing = mm3(key_up, key_down, mm_nt) * betas
    reach = jnp.where(reached, mm3(query_up, key_down, mm_nt), 0.0)
    inverse = (later == sooner).astype(F32)
    size = 1
    while size < tokens:
        pair = 2 * size
        corner = ((later // pair) == (sooner // pair)) & (later % pair >= size) & (sooner % pair < size)
        part = jnp.where(corner, mixing, 0.0)
        if size == 1:
            inverse = inverse - part
        else:
            inverse = inverse - mm3(mm3(inverse, part), inverse)
        size = pair
    spread = mm3(reach, inverse)
    coefficient = query_up - mm3(spread, betas * key_up)
    offset = mm3(spread, betas * values.astype(F32))
    return coefficient, offset


def routes(states, pages, me, side, rows, slots, pool_pages):
    n_z, n_y = side
    n_dp = n_z * n_y
    heads = states.shape[0]
    lanes = states.shape[1]
    kinds = heads + pages.shape[0]
    owners = jnp.concatenate([states // slots, pages // pool_pages], axis=0)
    head = lax.broadcasted_iota(jnp.int32, states.shape, 0)
    ids = jnp.concatenate(
        [head * slots + states % slots, heads * slots + pages % pool_pages], axis=0
    )
    here = owners == me
    first = jnp.min(jnp.where(here, ids, heads * slots + pool_pages - 1), axis=0, keepdims=True)
    second = jnp.max(jnp.where(here, ids, 0), axis=0, keepdims=True)
    span = 1
    while span < rows:
        first = jnp.minimum(first, pltpu.roll(first, lanes - span, 1))
        second = jnp.maximum(second, pltpu.roll(second, lanes - span, 1))
        span *= 2
    keys = owners * (heads * slots + pool_pages) + ids
    own = pltpu.roll(keys, (lanes - me * rows) % lanes, 1)[:, :LANES]
    place = lax.broadcasted_iota(jnp.int32, (1, LANES), 1)
    flat = jnp.zeros((1, LANES), jnp.int32)
    for kind in range(kinds):
        row = own[kind : kind + 1]
        if kind:
            row = pltpu.roll(row, kind * rows, 1)
        flat = jnp.where(place // rows == kind, row, flat)
    across = jnp.broadcast_to(flat, (LANES, LANES))
    down = jnp.transpose(across.astype(F32)).astype(jnp.int32)
    base = heads * slots + pool_pages
    valid = lax.broadcasted_iota(jnp.int32, (LANES, LANES), 0) < kinds * rows
    behind = valid & (down // base == across // base) & (down < across)
    late = jnp.max(behind.astype(F32), axis=0, keepdims=True).astype(jnp.int32)
    source = flat // base
    over_z = (me // n_y - source // n_y + n_z) % n_z
    over_y = (me % n_y - source % n_y + n_y) % n_y
    by_z = jnp.where(over_y == 0, 0, n_dp) + over_z * n_y + over_y
    by_y = jnp.where(over_z == 0, 0, n_dp) + over_y * n_z + over_z + 2 * n_dp
    return first, second, jnp.where(late == 0, by_z, by_y)


def fused(
    sizes,
    len_ref,
    state_table_ref,
    page_table_ref,
    states_ref,
    pages_ref,
    q_ref,
    k_ref,
    v_ref,
    gate_ref,
    beta_ref,
    mq_ref,
    new_ref,
    wuk_ref,
    wuv_ref,
    out_ref,
    records,
    q_buf,
    k_buf,
    v_buf,
    gate_buf,
    beta_buf,
    mq_buf,
    new_buf,
    wuk_buf,
    wuv_buf,
    state_slots,
    page_slots,
    picked_rows,
    place_row,
    picked,
    place,
    outgoing,
    incoming,
    lift_out,
    lift_in,
    wuv_in,
    page_out,
    context,
    result_out,
    coefs,
    offsets,
    tops,
    sums,
    mixes,
    send_sem,
    first_sem,
    second_sem,
    swap_send_sem,
    swap_recv_sem,
    lift_send_sem,
    lift_recv_sem,
    wuv_send_sem,
    wuv_recv_sem,
    back_send_sem,
    back_recv_sem,
    record_sem,
    load_sem,
    table_sem,
):
    n_z, n_y, n_t = sizes
    n_dp = n_z * n_y
    side = (n_z, n_y)
    recall_ref, mla_ref = out_ref.at[0], out_ref.at[1]
    heads, slots, hd, _ = states_ref.shape
    page_len, latent = pages_ref.shape[2], pages_ref.shape[3]
    rows, tokens, _ = q_ref.shape
    folds = latent // hd
    me = lax.axis_index("dp")
    mine = lax.axis_index("tensor")
    at_z, at_y = me // n_y, me % n_y

    n_local = heads * slots
    record_loads = [
        pltpu.make_async_copy(
            states_ref.at[h], records.at[pl.ds(h * slots, slots)], record_sem.at[h]
        )
        for h in range(heads)
    ] + [
        pltpu.make_async_copy(
            pages_ref.at[0, :, :, f * hd : (f + 1) * hd],
            records.at[pl.ds(n_local, pages_ref.shape[1]), f * page_len : (f + 1) * page_len, :],
            record_sem.at[heads + f],
        )
        for f in range(folds)
    ]
    loads = [
        pltpu.make_async_copy(source, target, load_sem.at[i])
        for i, (source, target) in enumerate(
            (
                (mq_ref, mq_buf),
                (wuk_ref, wuk_buf),
                (wuv_ref, wuv_buf),
                (q_ref, q_buf),
                (k_ref, k_buf),
                (v_ref, v_buf),
                (gate_ref, gate_buf),
                (beta_ref, beta_buf),
                (new_ref, new_buf),
            )
        )
    ]
    table_loads = [
        pltpu.make_async_copy(
            state_table_ref.at[pl.ds(pl.multiple_of(mine // 2 * (2 * heads), 2 * heads), 2 * heads)],
            state_slots,
            table_sem.at[0],
        ),
        pltpu.make_async_copy(page_table_ref.at[mine], page_slots, table_sem.at[1]),
    ]
    for load in table_loads + record_loads + loads:
        load.start()

    barrier = pltpu.get_barrier_semaphore()

    def greet_z(k, c):
        pl.semaphore_signal(barrier, inc=1, device_id={"dp": ((at_z + k) % n_z) * n_y + at_y})
        return c

    def greet_y(k, c):
        pl.semaphore_signal(barrier, inc=1, device_id={"dp": at_z * n_y + (at_y + k) % n_y})
        return c

    def greet_tensor(k, c):
        pl.semaphore_signal(barrier, inc=1, device_id={"tensor": (mine + k) % n_t})
        return c

    lax.fori_loop(1, n_z, greet_z, 0)
    lax.fori_loop(1, n_y, greet_y, 0)
    lax.fori_loop(1, n_t, greet_tensor, 0)

    for load in table_loads:
        load.wait()
    mine_slots = jnp.where(mine % 2 == 0, state_slots[0:heads, :], state_slots[heads : 2 * heads, :])
    first, second, slot = routes(
        mine_slots,
        page_slots[...],
        me,
        (n_z, n_y),
        rows,
        slots,
        pages_ref.shape[1],
    )
    picked_rows[0:1, :] = first
    picked_rows[1:2, :] = second
    place_row[...] = slot
    scalars = [
        pltpu.make_async_copy(picked_rows, picked, table_sem.at[2]),
        pltpu.make_async_copy(place_row, place, table_sem.at[3]),
    ]
    for load in scalars:
        load.start()
    for load in scalars + record_loads:
        load.wait()

    def hop(which, leg, k):
        along_z = which == leg
        if along_z:
            return {"dp": ((at_z + k) % n_z) * n_y + at_y}
        return {"dp": at_z * n_y + (at_y + k) % n_y}

    def stage(which, k, j):
        over_z, over_y = (k, j) if which == 0 else (j, k)
        target = ((at_z + over_z) % n_z) * n_y + (at_y + over_y) % n_y
        return records[picked[which, target * rows]]

    def nearest(i, n):
        return (((i + 1) // 2) * (1 - 2 * ((i + 1) % 2)) + n) % n

    def spot(which, leg, k, j):
        return ((2 * which + leg) * side[which] + k) * side[1 - which] + j

    def first_leg(which, k):
        return pltpu.make_async_remote_copy(
            src_ref=outgoing.at[which, k],
            dst_ref=incoming.at[pl.ds(spot(which, 0, k, 0), side[1 - which])],
            send_sem=send_sem.at[which, 0, k],
            recv_sem=first_sem.at[which, k],
            device_id=hop(which, 0, k),
        )

    def second_leg(which, k, j, own):
        held = outgoing.at[which, k, j] if own else incoming.at[spot(which, 0, k, j)]
        return pltpu.make_async_remote_copy(
            src_ref=held,
            dst_ref=incoming.at[spot(which, 1, k, j)],
            send_sem=send_sem.at[which, 1, j],
            recv_sem=second_sem.at[which, j],
            device_id=hop(which, 1, j),
        )

    def forward(which, k, own):
        n = side[1 - which]

        def one(i, c):
            second_leg(which, k, nearest(i, n), own).start()
            return c

        lax.fori_loop(1, n, one, 0)

    for which in range(2):
        incoming[spot(which, 0, 0, 0)] = stage(which, 0, 0)

    pl.semaphore_wait(barrier, n_z + n_y + n_t - 3)

    def send_first(which, k):
        for j in range(side[1 - which]):
            outgoing[which, k, j] = stage(which, k, j)
        first_leg(which, k).start()

    for which in range(2):
        for j in range(1, side[1 - which]):
            outgoing[which, 0, j] = stage(which, 0, j)
        forward(which, 0, True)
    for i in range(1, max(side)):
        for which in range(2):
            if i < side[which]:
                send_first(which, nearest(i, side[which]))

    for load in loads:
        load.wait()

    for h in range(heads):
        queries = mq_buf[:, :, h * hd : (h + 1) * hd].reshape(rows * tokens, hd)
        lifted = mm(queries, wuk_buf[h]).astype(BF16)
        lift_out[:, h] = lifted.reshape(rows, tokens, latent)
    lift_in[0] = lift_out[mine]
    wuv_in[0] = wuv_buf[...]

    def lift_copy(k):
        peer = (mine + k) % n_t
        return pltpu.make_async_remote_copy(
            src_ref=lift_out.at[peer],
            dst_ref=lift_in.at[n_t - k],
            send_sem=lift_send_sem.at[k],
            recv_sem=lift_recv_sem.at[n_t - k],
            device_id={"tensor": peer},
        )

    def wuv_copy(k):
        peer = (mine + k) % n_t
        return pltpu.make_async_remote_copy(
            src_ref=wuv_buf,
            dst_ref=wuv_in.at[n_t - k],
            send_sem=wuv_send_sem.at[k],
            recv_sem=wuv_recv_sem.at[n_t - k],
            device_id={"tensor": peer},
        )

    def page_copy(k):
        peer = (mine + k) % n_t
        return pltpu.make_async_remote_copy(
            src_ref=page_out.at[peer],
            dst_ref=context.at[n_t - k],
            send_sem=swap_send_sem.at[k],
            recv_sem=swap_recv_sem.at[n_t - k],
            device_id={"tensor": peer},
        )

    def back_copy(k):
        peer = (mine + k) % n_t
        return pltpu.make_async_remote_copy(
            src_ref=result_out.at[k],
            dst_ref=mla_ref.at[mine],
            send_sem=back_send_sem.at[k],
            recv_sem=back_recv_sem.at[n_t - k],
            device_id={"tensor": peer},
        )

    for k in range(1, n_t):
        lift_copy(k).start()
    for k in range(1, n_t):
        wuv_copy(k).start()

    def make_coefficients(r, c):
        alive = (
            lax.broadcasted_iota(jnp.int32, (heads * tokens, 1), 0) % tokens < len_ref[r]
        ).astype(F32)
        raw = beta_buf[r].astype(F32)
        raw = jnp.concatenate([raw[h : h + 1] for h in range(heads)], axis=1)
        square = (heads * tokens, heads * tokens)
        diagonal = lax.broadcasted_iota(jnp.int32, square, 0) == lax.broadcasted_iota(
            jnp.int32, square, 1
        )
        raw = jnp.sum(jnp.where(diagonal, raw, 0.0), axis=1, keepdims=True)
        betas = alive / (1.0 + jnp.exp(-raw))
        coefficient, offset = recall_coefficients(
            stack_heads(q_buf[r], heads, hd),
            stack_heads(k_buf[r], heads, hd),
            stack_heads(v_buf[r], heads, hd),
            stack_heads(gate_buf[r], heads, hd),
            betas,
            alive,
            tokens,
        )
        coefs[r] = coefficient
        offsets[r] = offset
        return c

    def pass_on(i, c):
        for which in range(2):
            k = nearest(i, side[which])
            first_leg(which, k).wait_recv()
            forward(which, k, False)
        return c

    def work(i, c):
        make_coefficients(i - 1, c)
        return pass_on(i, c)

    assert n_z == n_y
    paired = min(rows, n_z - 1)
    lax.fori_loop(1, paired + 1, work, 0)
    lax.fori_loop(paired + 1, n_z, pass_on, 0)
    lax.fori_loop(paired, rows, make_coefficients, 0)

    fresh = new_buf[mine]
    context[n_t] = jnp.concatenate(
        [fresh, jnp.zeros((context.shape[1] - tokens, latent), BF16)], axis=0
    )

    for which in range(2):
        for j in range(1, side[1 - which]):
            column = incoming.at[pl.ds(spot(which, 1, 0, 0), side[which])]
            pltpu.make_async_copy(column, column, second_sem.at[which, j]).wait()

    n_states = heads * rows

    def place_page(i, c):
        record = incoming[place[0, n_states + (i % pages_row) * rows + i // pages_row]]
        for f in range(folds):
            page_out[
                i // pages_row,
                pl.ds((i % pages_row) * page_len, page_len),
                f * hd : (f + 1) * hd,
            ] = record[f * page_len : (f + 1) * page_len]
        return c

    pages_row = page_out.shape[1] // page_len
    lax.fori_loop(0, rows * pages_row, place_page, 0)
    context[0] = page_out[mine]
    odd = mine % 2
    twin = 1 + (n_t - 2) * odd
    far = n_t // 4
    near_chips = [p for p in range(1, n_t // 2) if p != far]

    def cores(p):
        return (2 * p - odd, 2 * p + 1 - odd)

    page_copy(twin).start()
    for p in near_chips + [far]:
        for k in cores(p):
            page_copy(k).start()

    def recall(r, c):
        alive = (lax.broadcasted_iota(jnp.int32, (tokens, 1), 0) < len_ref[r]).astype(F32)
        for h in range(heads):
            state = incoming[place[0, h * rows + r]]
            high, low = halves(coefs[r, h * tokens : (h + 1) * tokens, :])
            both = mm(jnp.concatenate([high, low], axis=0), state)
            seen = both[:tokens] + both[tokens:] + offsets[r, h * tokens : (h + 1) * tokens, :]
            recall_ref[r, :, h * hd : (h + 1) * hd] = (seen * alive).astype(BF16)
        return c

    lax.fori_loop(0, rows, recall, 0)

    for k in range(1, n_t):
        lift_copy(k).wait_recv()
        wuv_copy(k).wait_recv()

    every = heads * tokens
    width = context.shape[1]
    group = 2
    size = group * every
    scale = hd ** (-0.5)
    column = lax.broadcasted_iota(jnp.int32, (size, width), 1)
    token = lax.broadcasted_iota(jnp.int32, (size, width), 0) % tokens
    row_alive = (lax.broadcasted_iota(jnp.int32, (tokens, 1), 0) < len_ref[mine]).astype(F32)

    def asked(i):
        return lift_in[i * group : (i + 1) * group].reshape(size, latent)

    def chip(p):
        return context[pl.ds(2 * p - odd, 2)].reshape(2 * width, latent)

    def arrive(k):
        page_copy(n_t - k).wait_recv()

    def fold(i, keys, masked=False, opened=True):
        span = slice(i * size, (i + 1) * size)
        parts = [mm_nt(asked(i), key) * scale for key in keys]
        if masked:
            parts[0] = jnp.where(column <= token, parts[0], -1e30)
        top = functools.reduce(
            jnp.maximum,
            [jnp.max(part, axis=-1, keepdims=True) for part in parts]
            + ([tops[span]] if opened else []),
        )
        parts = [jnp.exp(part - top) for part in parts]
        total = functools.reduce(
            jnp.add, [jnp.sum(part, axis=-1, keepdims=True) for part in parts]
        )
        mixed = functools.reduce(
            jnp.add, [mm(part.astype(BF16), key) for part, key in zip(parts, keys)]
        )
        if opened:
            fade = jnp.exp(tops[span] - top)
            total = total + fade * sums[span]
            mixed = mixed + fade * mixes[span]
        return span, top, total, mixed

    def keep(span, top, total, mixed):
        tops[span] = top
        sums[span] = total
        mixes[span] = mixed

    groups = n_t // group
    arrive(twin)
    for i in range(groups):
        keep(*fold(i, [context[n_t], context[0], context[twin]], masked=True, opened=False))
    for p in near_chips:
        for k in cores(p):
            arrive(k)
    if near_chips:
        for i in range(groups):
            keep(*fold(i, [chip(p) for p in near_chips]))

    for k in cores(far):
        arrive(k)
    for i in [*range(1, groups), 0]:
        _, _, total, mixed = fold(i, [chip(far)])
        attended = (mixed * (1.0 / total)).astype(BF16)
        for g in range(group):
            k = i * group + g
            for h in range(heads):
                first = (g * heads + h) * tokens
                out = mm(attended[first : first + tokens], wuv_in[k, h]) * row_alive
                result_out[k, :, h * hd : (h + 1) * hd] = out.astype(BF16)
            if k:
                back_copy(k).start()
    mla_ref[mine] = result_out[0]

    for k in range(1, n_t):
        back_copy(k).wait_recv()
    for k in range(1, n_t):
        lift_copy(k).wait_send()
        wuv_copy(k).wait_send()
        page_copy(k).wait_send()
        back_copy(k).wait_send()
    for which in range(2):
        for k in range(1, side[which]):
            first_leg(which, k).wait_send()
        for j in range(1, side[1 - which]):
            column = incoming.at[pl.ds(spot(which, 1, 0, 0), side[which])]
            pltpu.make_async_copy(column, column, send_sem.at[which, 1, j]).wait()


def run_fused(
    sizes,
    tool_len,
    state_table,
    page_table,
    kda_pool,
    latent_pool,
    kda_q,
    kda_k,
    kda_v,
    kda_gate,
    kda_beta,
    mla_q,
    mla_new,
    w_uk,
    w_uv,
):
    heads, slots, hd, _ = kda_pool.shape
    _, pool_pages, page_len, latent = latent_pool.shape
    rows, tokens, _ = kda_q.shape
    pages_row = pool_pages // rows
    n_z, n_y, n_t = sizes
    n_dp = n_z * n_y
    lanes = state_table.shape[1]
    vmem = pl.BlockSpec(memory_space=pltpu.VMEM)
    smem = pl.BlockSpec(memory_space=pltpu.SMEM)
    out = pltpu.VMEM((2,) + kda_q.shape, BF16)
    dma = pltpu.SemaphoreType.DMA
    both = pl.pallas_call(
        functools.partial(fused, sizes),
        out_shape=out,
        in_specs=[smem] + [pl.BlockSpec(memory_space=pl.ANY)] * 13,
        out_specs=vmem,
        scratch_shapes=[
            pltpu.VMEM((heads * slots + pool_pages, hd, hd), BF16),
            pltpu.VMEM(kda_q.shape, BF16),
            pltpu.VMEM(kda_k.shape, BF16),
            pltpu.VMEM(kda_v.shape, BF16),
            pltpu.VMEM(kda_gate.shape, BF16),
            pltpu.VMEM(kda_beta.shape, BF16),
            pltpu.VMEM(mla_q.shape, BF16),
            pltpu.VMEM(mla_new.shape, BF16),
            pltpu.VMEM(w_uk.shape, BF16),
            pltpu.VMEM(w_uv.shape, BF16),
            pltpu.VMEM((2 * heads, lanes), jnp.int32),
            pltpu.VMEM(page_table.shape[1:], jnp.int32),
            pltpu.VMEM((2, lanes), jnp.int32),
            pltpu.VMEM((1, LANES), jnp.int32),
            pltpu.SMEM((2, lanes), jnp.int32),
            pltpu.SMEM((1, LANES), jnp.int32),
            pltpu.VMEM((2, n_z, n_y, hd, hd), BF16),
            pltpu.VMEM((4 * n_dp, hd, hd), BF16),
            pltpu.VMEM((rows, heads, tokens, latent), BF16),
            pltpu.VMEM((n_t, heads, tokens, latent), BF16),
            pltpu.VMEM((n_t, heads, latent, hd), BF16),
            pltpu.VMEM((rows, pages_row * page_len, latent), BF16),
            pltpu.VMEM((n_t + 1, pages_row * page_len, latent), BF16),
            pltpu.VMEM((n_t, tokens, heads * hd), BF16),
            pltpu.VMEM((rows, heads * tokens, hd), F32),
            pltpu.VMEM((rows, heads * tokens, hd), F32),
            pltpu.VMEM((n_t * heads * tokens, 1), F32),
            pltpu.VMEM((n_t * heads * tokens, 1), F32),
            pltpu.VMEM((n_t * heads * tokens, latent), F32),
            dma((2, 2, max(n_z, n_y))),
            dma((2, max(n_z, n_y))),
            dma((2, max(n_z, n_y))),
        ]
        + [dma((n_t,))] * 8
        + [dma((heads + latent // hd,)), dma((9,)), dma((4,))],
        compiler_params=pltpu.CompilerParams(
            collective_id=0, has_side_effects=True, vmem_limit_bytes=60 * 1024 * 1024
        ),
    )(
        tool_len,
        state_table,
        page_table,
        kda_pool,
        latent_pool,
        kda_q,
        kda_k,
        kda_v,
        kda_gate,
        kda_beta,
        mla_q,
        mla_new,
        w_uk,
        w_uv,
    )
    return both[0], both[1]


def local(
    tool_len,
    state_table,
    page_table,
    kda_pool,
    latent_pool,
    kda_q,
    kda_k,
    kda_v,
    kda_gate,
    kda_beta,
    mla_q,
    mla_new,
    w_uk,
    w_uv,
):
    n_dp, n_t = lax.axis_size("dp"), lax.axis_size("tensor")
    return run_fused(
        (n_dp // SIDE_Y, SIDE_Y, n_t),
        tool_len,
        state_table.T,
        jnp.transpose(page_table, (1, 2, 0)),
        kda_pool,
        latent_pool,
        kda_q,
        kda_k,
        kda_v,
        kda_gate,
        jnp.transpose(kda_beta, (0, 2, 1)),
        mla_q,
        mla_new,
        w_uk,
        w_uv,
    )


def solution(mesh):
    in_specs = (
        P("dp"),
        P(),
        P(),
        P("tensor", "dp", None, None),
        P("tensor", "dp", None, None),
        P("dp", None, "tensor"),
        P("dp", None, "tensor"),
        P("dp", None, "tensor"),
        P("dp", None, "tensor"),
        P("dp", None, "tensor"),
        P("dp", None, "tensor"),
        P("dp", None, None),
        P("tensor", None, None),
        P("tensor", None, None),
    )
    out_specs = (P("dp", None, "tensor"), P("dp", None, "tensor"))
    return jax.shard_map(local, mesh=mesh, in_specs=in_specs, out_specs=out_specs, check_vma=False)
```

```python
import functools

import jax
import jax.numpy as jnp
from jax import lax
from jax.experimental import pallas as pl
from jax.experimental.pallas import tpu as pltpu
from jax.sharding import PartitionSpec as P

EPSILON = 1e-06
F32 = jnp.float32
BF16 = jnp.bfloat16
LANES = 128
SIDE_Y = 8


def mm(a, b):
    return lax.dot_general(a, b, (((1,), (0,)), ((), ())), preferred_element_type=F32)


def mm_nt(a, b):
    return lax.dot_general(a, b, (((1,), (1,)), ((), ())), preferred_element_type=F32)


def halves(values):
    high = values.astype(BF16)
    return high, (values - high.astype(F32)).astype(BF16)


def mm3(a, b, dot=mm):
    a_high, a_low = halves(a)
    b_high, b_low = halves(b)
    return dot(a_high, b_high) + (dot(a_high, b_low) + dot(a_low, b_high))


def unit_norm(values):
    return values / jnp.sqrt(jnp.sum(values * values, axis=-1, keepdims=True) + EPSILON)


def stack_heads(block, heads, width):
    return jnp.concatenate([block[:, h * width : (h + 1) * width] for h in range(heads)], axis=0)


def recall_coefficients(queries, keys, values, gates, betas, alive, tokens):
    rows = queries.shape[0]
    later = lax.broadcasted_iota(jnp.int32, (rows, rows), 0)
    sooner = lax.broadcasted_iota(jnp.int32, (rows, rows), 1)
    same = (later // tokens) == (sooner // tokens)
    reached = same & (sooner <= later)
    summed = mm(reached.astype(F32).astype(BF16), (gates.astype(F32) * alive).astype(BF16))
    grown = jnp.exp(summed)
    key_n = unit_norm(keys.astype(F32))
    query_up = unit_norm(queries.astype(F32)) * grown
    key_up = key_n * grown
    key_down = key_n * jnp.exp(-summed)
    mixing = mm3(key_up, key_down, mm_nt) * betas
    reach = jnp.where(reached, mm3(query_up, key_down, mm_nt), 0.0)
    inverse = (later == sooner).astype(F32)
    size = 1
    while size < tokens:
        pair = 2 * size
        corner = ((later // pair) == (sooner // pair)) & (later % pair >= size) & (sooner % pair < size)
        part = jnp.where(corner, mixing, 0.0)
        if size == 1:
            inverse = inverse - part
        else:
            inverse = inverse - mm3(mm3(inverse, part), inverse)
        size = pair
    spread = mm3(reach, inverse)
    coefficient = query_up - mm3(spread, betas * key_up)
    offset = mm3(spread, betas * values.astype(F32))
    return coefficient, offset


def routes(states, pages, me, side, rows, slots, pool_pages):
    n_z, n_y = side
    n_dp = n_z * n_y
    heads = states.shape[0]
    lanes = states.shape[1]
    kinds = heads + pages.shape[0]
    owners = jnp.concatenate([states // slots, pages // pool_pages], axis=0)
    head = lax.broadcasted_iota(jnp.int32, states.shape, 0)
    ids = jnp.concatenate(
        [head * slots + states % slots, heads * slots + pages % pool_pages], axis=0
    )
    here = owners == me
    first = jnp.min(jnp.where(here, ids, heads * slots + pool_pages - 1), axis=0, keepdims=True)
    second = jnp.max(jnp.where(here, ids, 0), axis=0, keepdims=True)
    span = 1
    while span < rows:
        first = jnp.minimum(first, pltpu.roll(first, lanes - span, 1))
        second = jnp.maximum(second, pltpu.roll(second, lanes - span, 1))
        span *= 2
    keys = owners * (heads * slots + pool_pages) + ids
    own = pltpu.roll(keys, (lanes - me * rows) % lanes, 1)[:, :LANES]
    place = lax.broadcasted_iota(jnp.int32, (1, LANES), 1)
    flat = jnp.zeros((1, LANES), jnp.int32)
    for kind in range(kinds):
        row = own[kind : kind + 1]
        if kind:
            row = pltpu.roll(row, kind * rows, 1)
        flat = jnp.where(place // rows == kind, row, flat)
    across = jnp.broadcast_to(flat, (LANES, LANES))
    down = jnp.transpose(across.astype(F32)).astype(jnp.int32)
    base = heads * slots + pool_pages
    valid = lax.broadcasted_iota(jnp.int32, (LANES, LANES), 0) < kinds * rows
    behind = valid & (down // base == across // base) & (down < across)
    late = jnp.max(behind.astype(F32), axis=0, keepdims=True).astype(jnp.int32)
    source = flat // base
    over_z = (me // n_y - source // n_y + n_z) % n_z
    over_y = (me % n_y - source % n_y + n_y) % n_y
    by_z = jnp.where(over_y == 0, 0, n_dp) + over_z * n_y + over_y
    by_y = jnp.where(over_z == 0, 0, n_dp) + over_y * n_z + over_z + 2 * n_dp
    return first, second, jnp.where(late == 0, by_z, by_y)


def fused(
    sizes,
    len_ref,
    state_table_ref,
    page_table_ref,
    states_ref,
    pages_ref,
    q_ref,
    k_ref,
    v_ref,
    gate_ref,
    beta_ref,
    mq_ref,
    new_ref,
    wuk_ref,
    wuv_ref,
    out_ref,
    records,
    q_buf,
    k_buf,
    v_buf,
    gate_buf,
    beta_buf,
    mq_buf,
    new_buf,
    wuk_buf,
    wuv_buf,
    state_slots,
    page_slots,
    picked_rows,
    place_row,
    picked,
    place,
    outgoing,
    incoming,
    lift_out,
    lift_in,
    wuv_in,
    page_out,
    context,
    result_out,
    coefs,
    offsets,
    tops,
    sums,
    mixes,
    send_sem,
    first_sem,
    second_sem,
    swap_send_sem,
    swap_recv_sem,
    lift_send_sem,
    lift_recv_sem,
    wuv_send_sem,
    wuv_recv_sem,
    back_send_sem,
    back_recv_sem,
    record_sem,
    load_sem,
    table_sem,
):
    n_z, n_y, n_t = sizes
    n_dp = n_z * n_y
    side = (n_z, n_y)
    recall_ref, mla_ref = out_ref.at[0], out_ref.at[1]
    heads, slots, hd, _ = states_ref.shape
    page_len, latent = pages_ref.shape[2], pages_ref.shape[3]
    rows, tokens, _ = q_ref.shape
    folds = latent // hd
    me = lax.axis_index("dp")
    mine = lax.axis_index("tensor")
    at_z, at_y = me // n_y, me % n_y

    n_local = heads * slots
    record_loads = [
        pltpu.make_async_copy(
            states_ref.at[h], records.at[pl.ds(h * slots, slots)], record_sem.at[h]
        )
        for h in range(heads)
    ] + [
        pltpu.make_async_copy(
            pages_ref.at[0, :, :, f * hd : (f + 1) * hd],
            records.at[pl.ds(n_local, pages_ref.shape[1]), f * page_len : (f + 1) * page_len, :],
            record_sem.at[heads + f],
        )
        for f in range(folds)
    ]
    loads = [
        pltpu.make_async_copy(source, target, load_sem.at[i])
        for i, (source, target) in enumerate(
            (
                (mq_ref, mq_buf),
                (wuk_ref, wuk_buf),
                (q_ref, q_buf),
                (k_ref, k_buf),
                (v_ref, v_buf),
                (gate_ref, gate_buf),
                (beta_ref, beta_buf),
                (new_ref, new_buf),
            )
        )
    ]
    table_loads = [
        pltpu.make_async_copy(
            state_table_ref.at[pl.ds(pl.multiple_of(mine // 2 * (2 * heads), 2 * heads), 2 * heads)],
            state_slots,
            table_sem.at[0],
        ),
        pltpu.make_async_copy(page_table_ref.at[mine], page_slots, table_sem.at[1]),
    ]
    loads += [
        pltpu.make_async_copy(
            wuv_ref.at[h], wuv_buf.at[:, h * hd : (h + 1) * hd], load_sem.at[len(loads) + h]
        )
        for h in range(heads)
    ]
    for load in table_loads + record_loads:
        load.start()

    barrier = pltpu.get_barrier_semaphore()

    def greet_z(k, c):
        pl.semaphore_signal(barrier, inc=1, device_id={"dp": ((at_z + k) % n_z) * n_y + at_y})
        return c

    def greet_y(k, c):
        pl.semaphore_signal(barrier, inc=1, device_id={"dp": at_z * n_y + (at_y + k) % n_y})
        return c

    def greet_tensor(k, c):
        pl.semaphore_signal(barrier, inc=1, device_id={"tensor": (mine + k) % n_t})
        return c

    lax.fori_loop(1, n_z, greet_z, 0)
    lax.fori_loop(1, n_y, greet_y, 0)
    lax.fori_loop(1, n_t, greet_tensor, 0)
    for load in loads:
        load.start()

    for load in table_loads:
        load.wait()
    mine_slots = jnp.where(mine % 2 == 0, state_slots[0:heads, :], state_slots[heads : 2 * heads, :])
    first, second, slot = routes(
        mine_slots,
        page_slots[...],
        me,
        (n_z, n_y),
        rows,
        slots,
        pages_ref.shape[1],
    )
    picked_rows[0:1, :] = first
    picked_rows[1:2, :] = second
    place_row[...] = slot
    scalars = [
        pltpu.make_async_copy(picked_rows, picked, table_sem.at[2]),
        pltpu.make_async_copy(place_row, place, table_sem.at[3]),
    ]
    for load in scalars:
        load.start()
    for load in scalars + record_loads:
        load.wait()

    def hop(which, leg, k):
        along_z = which == leg
        if along_z:
            return {"dp": ((at_z + k) % n_z) * n_y + at_y}
        return {"dp": at_z * n_y + (at_y + k) % n_y}

    def stage(which, k, j):
        over_z, over_y = (k, j) if which == 0 else (j, k)
        target = ((at_z + over_z) % n_z) * n_y + (at_y + over_y) % n_y
        return records[picked[which, target * rows]]

    def nearest(i, n):
        return (((i + 1) // 2) * (1 - 2 * ((i + 1) % 2)) + n) % n

    def spot(which, leg, k, j):
        return ((2 * which + leg) * side[which] + k) * side[1 - which] + j

    def first_leg(which, k):
        return pltpu.make_async_remote_copy(
            src_ref=outgoing.at[which, k],
            dst_ref=incoming.at[pl.ds(spot(which, 0, k, 0), side[1 - which])],
            send_sem=send_sem.at[which, 0, k],
            recv_sem=first_sem.at[which, k],
            device_id=hop(which, 0, k),
        )

    def second_leg(which, k, j, own):
        held = outgoing.at[which, k, j] if own else incoming.at[spot(which, 0, k, j)]
        return pltpu.make_async_remote_copy(
            src_ref=held,
            dst_ref=incoming.at[spot(which, 1, k, j)],
            send_sem=send_sem.at[which, 1, j],
            recv_sem=second_sem.at[which, j],
            device_id=hop(which, 1, j),
        )

    def forward(which, k, own):
        n = side[1 - which]

        def one(i, c):
            second_leg(which, k, nearest(i, n), own).start()
            return c

        lax.fori_loop(1, n, one, 0)

    for which in range(2):
        incoming[spot(which, 0, 0, 0)] = stage(which, 0, 0)

    pl.semaphore_wait(barrier, n_z + n_y + n_t - 3)

    def send_first(which, k):
        for j in range(side[1 - which]):
            outgoing[which, k, j] = stage(which, k, j)
        first_leg(which, k).start()

    for which in range(2):
        for j in range(1, side[1 - which]):
            outgoing[which, 0, j] = stage(which, 0, j)
        forward(which, 0, True)
    for i in range(1, max(side)):
        for which in range(2):
            if i < side[which]:
                send_first(which, nearest(i, side[which]))

    for load in loads:
        load.wait()

    for h in range(heads):
        queries = mq_buf[:, :, h * hd : (h + 1) * hd].reshape(rows * tokens, hd)
        lifted = mm(queries, wuk_buf[h]).astype(BF16)
        lift_out[:, h] = lifted.reshape(rows, tokens, latent)
    lift_in[0] = lift_out[mine]
    wuv_in[0] = wuv_buf[...]

    def lift_copy(k):
        peer = (mine + k) % n_t
        return pltpu.make_async_remote_copy(
            src_ref=lift_out.at[peer],
            dst_ref=lift_in.at[n_t - k],
            send_sem=lift_send_sem.at[k],
            recv_sem=lift_recv_sem.at[n_t - k],
            device_id={"tensor": peer},
        )

    def wuv_copy(k):
        peer = (mine + k) % n_t
        return pltpu.make_async_remote_copy(
            src_ref=wuv_buf,
            dst_ref=wuv_in.at[n_t - k],
            send_sem=wuv_send_sem.at[k],
            recv_sem=wuv_recv_sem.at[n_t - k],
            device_id={"tensor": peer},
        )

    def page_copy(k):
        peer = (mine + k) % n_t
        return pltpu.make_async_remote_copy(
            src_ref=page_out.at[peer],
            dst_ref=context.at[n_t - k],
            send_sem=swap_send_sem.at[k],
            recv_sem=swap_recv_sem.at[n_t - k],
            device_id={"tensor": peer},
        )

    def back_copy(k):
        peer = (mine + k) % n_t
        return pltpu.make_async_remote_copy(
            src_ref=result_out.at[k],
            dst_ref=mla_ref.at[mine],
            send_sem=back_send_sem.at[k],
            recv_sem=back_recv_sem.at[n_t - k],
            device_id={"tensor": peer},
        )

    for k in range(1, n_t):
        lift_copy(k).start()
    for k in range(1, n_t):
        wuv_copy(k).start()

    def make_coefficients(r, c):
        alive = (
            lax.broadcasted_iota(jnp.int32, (heads * tokens, 1), 0) % tokens < len_ref[r]
        ).astype(F32)
        raw = beta_buf[r].astype(F32)
        raw = jnp.concatenate([raw[h : h + 1] for h in range(heads)], axis=1)
        square = (heads * tokens, heads * tokens)
        diagonal = lax.broadcasted_iota(jnp.int32, square, 0) == lax.broadcasted_iota(
            jnp.int32, square, 1
        )
        raw = jnp.sum(jnp.where(diagonal, raw, 0.0), axis=1, keepdims=True)
        betas = alive / (1.0 + jnp.exp(-raw))
        coefficient, offset = recall_coefficients(
            stack_heads(q_buf[r], heads, hd),
            stack_heads(k_buf[r], heads, hd),
            stack_heads(v_buf[r], heads, hd),
            stack_heads(gate_buf[r], heads, hd),
            betas,
            alive,
            tokens,
        )
        coefs[r] = coefficient
        offsets[r] = offset
        return c

    def pass_on(i, c):
        for which in range(2):
            k = nearest(i, side[which])
            first_leg(which, k).wait_recv()
            forward(which, k, False)
        return c

    def work(i, c):
        make_coefficients(i - 1, c)
        return pass_on(i, c)

    assert n_z == n_y
    paired = min(rows, n_z - 1)
    lax.fori_loop(1, paired + 1, work, 0)
    lax.fori_loop(paired + 1, n_z, pass_on, 0)
    lax.fori_loop(paired, rows, make_coefficients, 0)

    fresh = new_buf[mine]
    context[n_t] = jnp.concatenate(
        [fresh, jnp.zeros((context.shape[1] - tokens, latent), BF16)], axis=0
    )

    for which in range(2):
        for j in range(1, side[1 - which]):
            column = incoming.at[pl.ds(spot(which, 1, 0, 0), side[which])]
            pltpu.make_async_copy(column, column, second_sem.at[which, j]).wait()

    n_states = heads * rows

    def place_page(i, c):
        record = incoming[place[0, n_states + (i % pages_row) * rows + i // pages_row]]
        for f in range(folds):
            page_out[
                i // pages_row,
                pl.ds((i % pages_row) * page_len, page_len),
                f * hd : (f + 1) * hd,
            ] = record[f * page_len : (f + 1) * page_len]
        return c

    pages_row = page_out.shape[1] // page_len
    lax.fori_loop(0, rows * pages_row, place_page, 0)
    context[0] = page_out[mine]
    odd = mine % 2
    twin = 1 + (n_t - 2) * odd
    far = n_t // 4
    near_chips = [p for p in range(1, n_t // 2) if p != far]

    def cores(p):
        return (2 * p - odd, 2 * p + 1 - odd)

    page_copy(twin).start()
    for p in near_chips + [far]:
        for k in cores(p):
            page_copy(k).start()

    def recall(r, c):
        alive = (lax.broadcasted_iota(jnp.int32, (tokens, 1), 0) < len_ref[r]).astype(F32)
        for h in range(heads):
            state = incoming[place[0, h * rows + r]]
            high, low = halves(coefs[r, h * tokens : (h + 1) * tokens, :])
            both = mm(jnp.concatenate([high, low], axis=0), state)
            seen = both[:tokens] + both[tokens:] + offsets[r, h * tokens : (h + 1) * tokens, :]
            recall_ref[r, :, h * hd : (h + 1) * hd] = (seen * alive).astype(BF16)
        return c

    lax.fori_loop(0, rows, recall, 0)

    for k in range(1, n_t):
        lift_copy(k).wait_recv()
        wuv_copy(k).wait_recv()

    every = heads * tokens
    width = context.shape[1]
    group = 2
    size = group * every
    scale = hd ** (-0.5)
    column = lax.broadcasted_iota(jnp.int32, (size, width), 1)
    token = lax.broadcasted_iota(jnp.int32, (size, width), 0) % tokens
    row_alive = (lax.broadcasted_iota(jnp.int32, (tokens, 1), 0) < len_ref[mine]).astype(F32)

    def asked(i):
        return lift_in[i * group : (i + 1) * group].reshape(size, latent)

    def chip(p):
        return context[pl.ds(2 * p - odd, 2)].reshape(2 * width, latent)

    def arrive(k):
        page_copy(n_t - k).wait_recv()

    def fold(i, keys, masked=False, opened=True):
        span = slice(i * size, (i + 1) * size)
        parts = [mm_nt(asked(i), key) * scale for key in keys]
        if masked:
            parts[0] = jnp.where(column <= token, parts[0], -1e30)
        top = functools.reduce(
            jnp.maximum,
            [jnp.max(part, axis=-1, keepdims=True) for part in parts]
            + ([tops[span]] if opened else []),
        )
        parts = [jnp.exp(part - top) for part in parts]
        total = functools.reduce(
            jnp.add, [jnp.sum(part, axis=-1, keepdims=True) for part in parts]
        )
        mixed = functools.reduce(
            jnp.add, [mm(part.astype(BF16), key) for part, key in zip(parts, keys)]
        )
        if opened:
            fade = jnp.exp(tops[span] - top)
            total = total + fade * sums[span]
            mixed = mixed + fade * mixes[span]
        return span, top, total, mixed

    def keep(span, top, total, mixed):
        tops[span] = top
        sums[span] = total
        mixes[span] = mixed

    groups = n_t // group
    arrive(twin)
    for i in range(groups):
        keep(*fold(i, [context[n_t], context[0], context[twin]], masked=True, opened=False))
    for p in near_chips:
        for k in cores(p):
            arrive(k)
    if near_chips:
        for i in range(groups):
            keep(*fold(i, [chip(p) for p in near_chips]))

    for k in cores(far):
        arrive(k)
    for i in [*range(groups // 2, groups), *range(1, groups // 2), 0]:
        _, _, total, mixed = fold(i, [chip(far)])
        attended = (mixed * (1.0 / total)).astype(BF16)
        for g in range(group):
            k = i * group + g
            out = mm(attended[g * every : (g + 1) * every], wuv_in[k])
            for h in range(heads):
                own = out[h * tokens : (h + 1) * tokens, h * hd : (h + 1) * hd] * row_alive
                result_out[k, :, h * hd : (h + 1) * hd] = own.astype(BF16)
            if k:
                back_copy(k).start()
    mla_ref[mine] = result_out[0]

    for k in range(1, n_t):
        back_copy(k).wait_recv()
    for k in range(1, n_t):
        lift_copy(k).wait_send()
        wuv_copy(k).wait_send()
        page_copy(k).wait_send()
        back_copy(k).wait_send()
    for which in range(2):
        for k in range(1, side[which]):
            first_leg(which, k).wait_send()
        for j in range(1, side[1 - which]):
            column = incoming.at[pl.ds(spot(which, 1, 0, 0), side[which])]
            pltpu.make_async_copy(column, column, send_sem.at[which, 1, j]).wait()


def run_fused(
    sizes,
    tool_len,
    state_table,
    page_table,
    kda_pool,
    latent_pool,
    kda_q,
    kda_k,
    kda_v,
    kda_gate,
    kda_beta,
    mla_q,
    mla_new,
    w_uk,
    w_uv,
):
    heads, slots, hd, _ = kda_pool.shape
    _, pool_pages, page_len, latent = latent_pool.shape
    rows, tokens, _ = kda_q.shape
    pages_row = pool_pages // rows
    n_z, n_y, n_t = sizes
    n_dp = n_z * n_y
    lanes = state_table.shape[1]
    vmem = pl.BlockSpec(memory_space=pltpu.VMEM)
    smem = pl.BlockSpec(memory_space=pltpu.SMEM)
    out = pltpu.VMEM((2,) + kda_q.shape, BF16)
    dma = pltpu.SemaphoreType.DMA
    both = pl.pallas_call(
        functools.partial(fused, sizes),
        out_shape=out,
        in_specs=[smem] + [pl.BlockSpec(memory_space=pl.ANY)] * 13,
        out_specs=vmem,
        scratch_shapes=[
            pltpu.VMEM((heads * slots + pool_pages, hd, hd), BF16),
            pltpu.VMEM(kda_q.shape, BF16),
            pltpu.VMEM(kda_k.shape, BF16),
            pltpu.VMEM(kda_v.shape, BF16),
            pltpu.VMEM(kda_gate.shape, BF16),
            pltpu.VMEM(kda_beta.shape, BF16),
            pltpu.VMEM(mla_q.shape, BF16),
            pltpu.VMEM(mla_new.shape, BF16),
            pltpu.VMEM(w_uk.shape, BF16),
            pltpu.VMEM((latent, heads * hd), BF16),
            pltpu.VMEM((2 * heads, lanes), jnp.int32),
            pltpu.VMEM(page_table.shape[1:], jnp.int32),
            pltpu.VMEM((2, lanes), jnp.int32),
            pltpu.VMEM((1, LANES), jnp.int32),
            pltpu.SMEM((2, lanes), jnp.int32),
            pltpu.SMEM((1, LANES), jnp.int32),
            pltpu.VMEM((2, n_z, n_y, hd, hd), BF16),
            pltpu.VMEM((4 * n_dp, hd, hd), BF16),
            pltpu.VMEM((rows, heads, tokens, latent), BF16),
            pltpu.VMEM((n_t, heads, tokens, latent), BF16),
            pltpu.VMEM((n_t, latent, heads * hd), BF16),
            pltpu.VMEM((rows, pages_row * page_len, latent), BF16),
            pltpu.VMEM((n_t + 1, pages_row * page_len, latent), BF16),
            pltpu.VMEM((n_t, tokens, heads * hd), BF16),
            pltpu.VMEM((rows, heads * tokens, hd), F32),
            pltpu.VMEM((rows, heads * tokens, hd), F32),
            pltpu.VMEM((n_t * heads * tokens, 1), F32),
            pltpu.VMEM((n_t * heads * tokens, 1), F32),
            pltpu.VMEM((n_t * heads * tokens, latent), F32),
            dma((2, 2, max(n_z, n_y))),
            dma((2, max(n_z, n_y))),
            dma((2, max(n_z, n_y))),
        ]
        + [dma((n_t,))] * 8
        + [dma((heads + latent // hd,)), dma((8 + heads,)), dma((4,))],
        compiler_params=pltpu.CompilerParams(
            collective_id=0, has_side_effects=True, vmem_limit_bytes=60 * 1024 * 1024
        ),
    )(
        tool_len,
        state_table,
        page_table,
        kda_pool,
        latent_pool,
        kda_q,
        kda_k,
        kda_v,
        kda_gate,
        kda_beta,
        mla_q,
        mla_new,
        w_uk,
        w_uv,
    )
    return both[0], both[1]


def local(
    tool_len,
    state_table,
    page_table,
    kda_pool,
    latent_pool,
    kda_q,
    kda_k,
    kda_v,
    kda_gate,
    kda_beta,
    mla_q,
    mla_new,
    w_uk,
    w_uv,
):
    n_dp, n_t = lax.axis_size("dp"), lax.axis_size("tensor")
    return run_fused(
        (n_dp // SIDE_Y, SIDE_Y, n_t),
        tool_len,
        state_table.T,
        jnp.transpose(page_table, (1, 2, 0)),
        kda_pool,
        latent_pool,
        kda_q,
        kda_k,
        kda_v,
        kda_gate,
        jnp.transpose(kda_beta, (0, 2, 1)),
        mla_q,
        mla_new,
        w_uk,
        w_uv,
    )


def solution(mesh):
    in_specs = (
        P("dp"),
        P(),
        P(),
        P("tensor", "dp", None, None),
        P("tensor", "dp", None, None),
        P("dp", None, "tensor"),
        P("dp", None, "tensor"),
        P("dp", None, "tensor"),
        P("dp", None, "tensor"),
        P("dp", None, "tensor"),
        P("dp", None, "tensor"),
        P("dp", None, None),
        P("tensor", None, None),
        P("tensor", None, None),
    )
    out_specs = (P("dp", None, "tensor"), P("dp", None, "tensor"))
    return jax.shard_map(local, mesh=mesh, in_specs=in_specs, out_specs=out_specs, check_vma=False)
```

```python
import functools

import jax
import jax.numpy as jnp
from jax import lax
from jax.experimental import pallas as pl
from jax.experimental.pallas import tpu as pltpu
from jax.sharding import PartitionSpec as P

EPSILON = 1e-06
F32 = jnp.float32
BF16 = jnp.bfloat16
LANES = 128
SIDE_Y = 8


def mm(a, b):
    return lax.dot_general(a, b, (((1,), (0,)), ((), ())), preferred_element_type=F32)


def mm_nt(a, b):
    return lax.dot_general(a, b, (((1,), (1,)), ((), ())), preferred_element_type=F32)


def halves(values):
    high = values.astype(BF16)
    return high, (values - high.astype(F32)).astype(BF16)


def mm3(a, b, dot=mm):
    a_high, a_low = halves(a)
    b_high, b_low = halves(b)
    return dot(a_high, b_high) + (dot(a_high, b_low) + dot(a_low, b_high))


def unit_norm(values):
    return values / jnp.sqrt(jnp.sum(values * values, axis=-1, keepdims=True) + EPSILON)


def stack_heads(block, heads, width):
    return jnp.concatenate([block[:, h * width : (h + 1) * width] for h in range(heads)], axis=0)


def recall_coefficients(queries, keys, values, gates, betas, alive, tokens):
    rows = queries.shape[0]
    later = lax.broadcasted_iota(jnp.int32, (rows, rows), 0)
    sooner = lax.broadcasted_iota(jnp.int32, (rows, rows), 1)
    same = (later // tokens) == (sooner // tokens)
    reached = same & (sooner <= later)
    summed = mm(reached.astype(F32).astype(BF16), (gates.astype(F32) * alive).astype(BF16))
    grown = jnp.exp(summed)
    key_n = unit_norm(keys.astype(F32))
    query_up = unit_norm(queries.astype(F32)) * grown
    key_up = key_n * grown
    key_down = key_n * jnp.exp(-summed)
    mixing = mm3(key_up, key_down, mm_nt) * betas
    reach = jnp.where(reached, mm3(query_up, key_down, mm_nt), 0.0)
    inverse = (later == sooner).astype(F32)
    size = 1
    while size < tokens:
        pair = 2 * size
        corner = ((later // pair) == (sooner // pair)) & (later % pair >= size) & (sooner % pair < size)
        part = jnp.where(corner, mixing, 0.0)
        if size == 1:
            inverse = inverse - part
        else:
            inverse = inverse - mm3(mm3(inverse, part), inverse)
        size = pair
    spread = mm3(reach, inverse)
    coefficient = query_up - mm3(spread, betas * key_up)
    offset = mm3(spread, betas * values.astype(F32))
    return coefficient, offset


def routes(states, pages, me, side, rows, slots, pool_pages):
    n_z, n_y = side
    n_dp = n_z * n_y
    heads = states.shape[0]
    lanes = states.shape[1]
    kinds = heads + pages.shape[0]
    owners = jnp.concatenate([states // slots, pages // pool_pages], axis=0)
    head = lax.broadcasted_iota(jnp.int32, states.shape, 0)
    ids = jnp.concatenate(
        [head * slots + states % slots, heads * slots + pages % pool_pages], axis=0
    )
    here = owners == me
    first = jnp.min(jnp.where(here, ids, heads * slots + pool_pages - 1), axis=0, keepdims=True)
    second = jnp.max(jnp.where(here, ids, 0), axis=0, keepdims=True)
    span = 1
    while span < rows:
        first = jnp.minimum(first, pltpu.roll(first, lanes - span, 1))
        second = jnp.maximum(second, pltpu.roll(second, lanes - span, 1))
        span *= 2
    keys = owners * (heads * slots + pool_pages) + ids
    own = pltpu.roll(keys, (lanes - me * rows) % lanes, 1)[:, :LANES]
    place = lax.broadcasted_iota(jnp.int32, (1, LANES), 1)
    flat = jnp.zeros((1, LANES), jnp.int32)
    for kind in range(kinds):
        row = own[kind : kind + 1]
        if kind:
            row = pltpu.roll(row, kind * rows, 1)
        flat = jnp.where(place // rows == kind, row, flat)
    across = jnp.broadcast_to(flat, (LANES, LANES))
    down = jnp.transpose(across.astype(F32)).astype(jnp.int32)
    base = heads * slots + pool_pages
    valid = lax.broadcasted_iota(jnp.int32, (LANES, LANES), 0) < kinds * rows
    behind = valid & (down // base == across // base) & (down < across)
    late = jnp.max(behind.astype(F32), axis=0, keepdims=True).astype(jnp.int32)
    source = flat // base
    over_z = (me // n_y - source // n_y + n_z) % n_z
    over_y = (me % n_y - source % n_y + n_y) % n_y
    by_z = jnp.where(over_y == 0, 0, n_dp) + over_z * n_y + over_y
    by_y = jnp.where(over_z == 0, 0, n_dp) + over_y * n_z + over_z + 2 * n_dp
    return first, second, jnp.where(late == 0, by_z, by_y)


def fused(
    sizes,
    len_ref,
    state_table_ref,
    page_table_ref,
    states_ref,
    pages_ref,
    q_ref,
    k_ref,
    v_ref,
    gate_ref,
    beta_ref,
    mq_ref,
    new_ref,
    wuk_ref,
    wuv_ref,
    out_ref,
    records,
    q_buf,
    k_buf,
    v_buf,
    gate_buf,
    beta_buf,
    mq_buf,
    new_buf,
    wuk_buf,
    wuv_buf,
    state_slots,
    page_slots,
    picked_rows,
    place_row,
    picked,
    place,
    outgoing,
    incoming,
    lift_out,
    lift_in,
    wuv_in,
    page_out,
    context,
    result_out,
    coefs,
    offsets,
    tops,
    sums,
    mixes,
    send_sem,
    first_sem,
    second_sem,
    swap_send_sem,
    swap_recv_sem,
    lift_send_sem,
    lift_recv_sem,
    wuv_send_sem,
    wuv_recv_sem,
    back_send_sem,
    back_recv_sem,
    record_sem,
    load_sem,
    table_sem,
):
    n_z, n_y, n_t = sizes
    n_dp = n_z * n_y
    side = (n_z, n_y)
    recall_ref, mla_ref = out_ref.at[0], out_ref.at[1]
    heads, slots, hd, _ = states_ref.shape
    page_len, latent = pages_ref.shape[2], pages_ref.shape[3]
    rows, tokens, _ = q_ref.shape
    folds = latent // hd
    me = lax.axis_index("dp")
    mine = lax.axis_index("tensor")
    at_z, at_y = me // n_y, me % n_y

    n_local = heads * slots
    record_loads = [
        pltpu.make_async_copy(
            states_ref.at[h], records.at[pl.ds(h * slots, slots)], record_sem.at[h]
        )
        for h in range(heads)
    ] + [
        pltpu.make_async_copy(
            pages_ref.at[0, :, :, f * hd : (f + 1) * hd],
            records.at[pl.ds(n_local, pages_ref.shape[1]), f * page_len : (f + 1) * page_len, :],
            record_sem.at[heads + f],
        )
        for f in range(folds)
    ]
    loads = [
        pltpu.make_async_copy(source, target, load_sem.at[i])
        for i, (source, target) in enumerate(
            (
                (mq_ref, mq_buf),
                (wuk_ref, wuk_buf),
                (q_ref, q_buf),
                (k_ref, k_buf),
                (v_ref, v_buf),
                (gate_ref, gate_buf),
                (beta_ref, beta_buf),
                (new_ref, new_buf),
            )
        )
    ]
    table_loads = [
        pltpu.make_async_copy(
            state_table_ref.at[pl.ds(pl.multiple_of(mine // 2 * (2 * heads), 2 * heads), 2 * heads)],
            state_slots,
            table_sem.at[0],
        ),
        pltpu.make_async_copy(page_table_ref.at[mine], page_slots, table_sem.at[1]),
    ]
    loads += [
        pltpu.make_async_copy(
            wuv_ref.at[h], wuv_buf.at[:, h * hd : (h + 1) * hd], load_sem.at[len(loads) + h]
        )
        for h in range(heads)
    ]
    for load in table_loads + record_loads:
        load.start()

    barrier = pltpu.get_barrier_semaphore()

    def greet_z(k, c):
        pl.semaphore_signal(barrier, inc=1, device_id={"dp": ((at_z + k) % n_z) * n_y + at_y})
        return c

    def greet_y(k, c):
        pl.semaphore_signal(barrier, inc=1, device_id={"dp": at_z * n_y + (at_y + k) % n_y})
        return c

    def greet_tensor(k, c):
        pl.semaphore_signal(barrier, inc=1, device_id={"tensor": (mine + k) % n_t})
        return c

    lax.fori_loop(1, n_z, greet_z, 0)
    lax.fori_loop(1, n_y, greet_y, 0)
    lax.fori_loop(1, n_t, greet_tensor, 0)
    for load in loads:
        load.start()

    for load in table_loads:
        load.wait()
    mine_slots = jnp.where(mine % 2 == 0, state_slots[0:heads, :], state_slots[heads : 2 * heads, :])
    first, second, slot = routes(
        mine_slots,
        page_slots[...],
        me,
        (n_z, n_y),
        rows,
        slots,
        pages_ref.shape[1],
    )
    picked_rows[0:1, :] = first
    picked_rows[1:2, :] = second
    place_row[...] = slot
    scalars = [
        pltpu.make_async_copy(picked_rows, picked, table_sem.at[2]),
        pltpu.make_async_copy(place_row, place, table_sem.at[3]),
    ]
    for load in scalars:
        load.start()
    for load in scalars + record_loads:
        load.wait()

    def hop(which, leg, k):
        along_z = which == leg
        if along_z:
            return {"dp": ((at_z + k) % n_z) * n_y + at_y}
        return {"dp": at_z * n_y + (at_y + k) % n_y}

    def stage(which, k, j):
        over_z, over_y = (k, j) if which == 0 else (j, k)
        target = ((at_z + over_z) % n_z) * n_y + (at_y + over_y) % n_y
        return records[picked[which, target * rows]]

    def nearest(i, n):
        return (((i + 1) // 2) * (1 - 2 * ((i + 1) % 2)) + n) % n

    def spot(which, leg, k, j):
        return ((2 * which + leg) * side[which] + k) * side[1 - which] + j

    def first_leg(which, k):
        return pltpu.make_async_remote_copy(
            src_ref=outgoing.at[which, k],
            dst_ref=incoming.at[pl.ds(spot(which, 0, k, 0), side[1 - which])],
            send_sem=send_sem.at[which, 0, k],
            recv_sem=first_sem.at[which, k],
            device_id=hop(which, 0, k),
        )

    def second_leg(which, k, j, own):
        held = outgoing.at[which, k, j] if own else incoming.at[spot(which, 0, k, j)]
        return pltpu.make_async_remote_copy(
            src_ref=held,
            dst_ref=incoming.at[spot(which, 1, k, j)],
            send_sem=send_sem.at[which, 1, j],
            recv_sem=second_sem.at[which, j],
            device_id=hop(which, 1, j),
        )

    def forward(which, k, own):
        n = side[1 - which]

        def one(i, c):
            second_leg(which, k, nearest(i, n), own).start()
            return c

        lax.fori_loop(1, n, one, 0)

    for which in range(2):
        incoming[spot(which, 0, 0, 0)] = stage(which, 0, 0)

    pl.semaphore_wait(barrier, n_z + n_y + n_t - 3)

    def send_first(which, k):
        for j in range(side[1 - which]):
            outgoing[which, k, j] = stage(which, k, j)
        first_leg(which, k).start()

    for which in range(2):
        for j in range(1, side[1 - which]):
            outgoing[which, 0, j] = stage(which, 0, j)
        forward(which, 0, True)
    for i in range(1, max(side)):
        for which in range(2):
            if i < side[which]:
                send_first(which, nearest(i, side[which]))

    for load in loads:
        load.wait()

    for h in range(heads):
        queries = mq_buf[:, :, h * hd : (h + 1) * hd].reshape(rows * tokens, hd)
        lifted = mm(queries, wuk_buf[h]).astype(BF16)
        lift_out[:, h] = lifted.reshape(rows, tokens, latent)
    lift_in[0] = lift_out[mine]
    wuv_in[0] = wuv_buf[...]

    def lift_copy(k):
        peer = (mine + k) % n_t
        return pltpu.make_async_remote_copy(
            src_ref=lift_out.at[peer],
            dst_ref=lift_in.at[n_t - k],
            send_sem=lift_send_sem.at[k],
            recv_sem=lift_recv_sem.at[n_t - k],
            device_id={"tensor": peer},
        )

    def wuv_copy(k):
        peer = (mine + k) % n_t
        return pltpu.make_async_remote_copy(
            src_ref=wuv_buf,
            dst_ref=wuv_in.at[n_t - k],
            send_sem=wuv_send_sem.at[k],
            recv_sem=wuv_recv_sem.at[n_t - k],
            device_id={"tensor": peer},
        )

    def page_copy(k):
        peer = (mine + k) % n_t
        return pltpu.make_async_remote_copy(
            src_ref=page_out.at[peer],
            dst_ref=context.at[n_t - k],
            send_sem=swap_send_sem.at[k],
            recv_sem=swap_recv_sem.at[n_t - k],
            device_id={"tensor": peer},
        )

    def back_copy(k):
        peer = (mine + k) % n_t
        return pltpu.make_async_remote_copy(
            src_ref=result_out.at[k],
            dst_ref=mla_ref.at[mine],
            send_sem=back_send_sem.at[k],
            recv_sem=back_recv_sem.at[n_t - k],
            device_id={"tensor": peer},
        )

    for k in range(1, n_t):
        lift_copy(k).start()
    for k in range(1, n_t):
        wuv_copy(k).start()

    def make_coefficients(r, c):
        alive = (
            lax.broadcasted_iota(jnp.int32, (heads * tokens, 1), 0) % tokens < len_ref[r]
        ).astype(F32)
        raw = beta_buf[r].astype(F32)
        raw = jnp.concatenate([raw[h : h + 1] for h in range(heads)], axis=1)
        square = (heads * tokens, heads * tokens)
        diagonal = lax.broadcasted_iota(jnp.int32, square, 0) == lax.broadcasted_iota(
            jnp.int32, square, 1
        )
        raw = jnp.sum(jnp.where(diagonal, raw, 0.0), axis=1, keepdims=True)
        betas = alive / (1.0 + jnp.exp(-raw))
        coefficient, offset = recall_coefficients(
            stack_heads(q_buf[r], heads, hd),
            stack_heads(k_buf[r], heads, hd),
            stack_heads(v_buf[r], heads, hd),
            stack_heads(gate_buf[r], heads, hd),
            betas,
            alive,
            tokens,
        )
        coefs[r] = coefficient
        offsets[r] = offset
        return c

    def pass_on(i, c):
        for which in range(2):
            k = nearest(i, side[which])
            first_leg(which, k).wait_recv()
            forward(which, k, False)
        return c

    def work(i, c):
        pass_on(i, c)
        return make_coefficients(i - 1, c)

    assert n_z == n_y
    paired = min(rows, n_z - 1)
    lax.fori_loop(1, paired + 1, work, 0)
    lax.fori_loop(paired + 1, n_z, pass_on, 0)
    lax.fori_loop(paired, rows, make_coefficients, 0)

    fresh = new_buf[mine]
    context[n_t] = jnp.concatenate(
        [fresh, jnp.zeros((context.shape[1] - tokens, latent), BF16)], axis=0
    )

    for which in range(2):
        for j in range(1, side[1 - which]):
            column = incoming.at[pl.ds(spot(which, 1, 0, 0), side[which])]
            pltpu.make_async_copy(column, column, second_sem.at[which, j]).wait()

    n_states = heads * rows

    def place_page(i, c):
        record = incoming[place[0, n_states + (i % pages_row) * rows + i // pages_row]]
        for f in range(folds):
            page_out[
                i // pages_row,
                pl.ds((i % pages_row) * page_len, page_len),
                f * hd : (f + 1) * hd,
            ] = record[f * page_len : (f + 1) * page_len]
        return c

    pages_row = page_out.shape[1] // page_len

    def place_row_of(r):
        lax.fori_loop(0, pages_row, lambda j, c: place_page(r * pages_row + j, c), 0)

    def hand_over(k):
        place_row_of((mine + k) % n_t)
        page_copy(k).start()

    odd = mine % 2
    twin = 1 + (n_t - 2) * odd
    far = n_t // 4
    near_chips = [p for p in range(1, n_t // 2) if p != far]

    def cores(p):
        return (2 * p - odd, 2 * p + 1 - odd)

    hand_over(twin)
    for p in near_chips + [far]:
        for k in cores(p):
            hand_over(k)
    place_row_of(mine)
    context[0] = page_out[mine]

    def recall(r, c):
        alive = (lax.broadcasted_iota(jnp.int32, (tokens, 1), 0) < len_ref[r]).astype(F32)
        for h in range(heads):
            state = incoming[place[0, h * rows + r]]
            high, low = halves(coefs[r, h * tokens : (h + 1) * tokens, :])
            both = mm(jnp.concatenate([high, low], axis=0), state)
            seen = both[:tokens] + both[tokens:] + offsets[r, h * tokens : (h + 1) * tokens, :]
            recall_ref[r, :, h * hd : (h + 1) * hd] = (seen * alive).astype(BF16)
        return c

    lax.fori_loop(0, rows, recall, 0)

    for k in range(1, n_t):
        lift_copy(k).wait_recv()
        wuv_copy(k).wait_recv()

    every = heads * tokens
    width = context.shape[1]
    group = 2
    size = group * every
    scale = hd ** (-0.5)
    column = lax.broadcasted_iota(jnp.int32, (size, width), 1)
    token = lax.broadcasted_iota(jnp.int32, (size, width), 0) % tokens
    row_alive = (lax.broadcasted_iota(jnp.int32, (tokens, 1), 0) < len_ref[mine]).astype(F32)

    def asked(i):
        return lift_in[i * group : (i + 1) * group].reshape(size, latent)

    def chip(p):
        return context[pl.ds(2 * p - odd, 2)].reshape(2 * width, latent)

    def arrive(k):
        page_copy(n_t - k).wait_recv()

    def fold(i, keys, masked=False, opened=True):
        span = slice(i * size, (i + 1) * size)
        parts = [mm_nt(asked(i), key) * scale for key in keys]
        if masked:
            parts[0] = jnp.where(column <= token, parts[0], -1e30)
        top = functools.reduce(
            jnp.maximum,
            [jnp.max(part, axis=-1, keepdims=True) for part in parts]
            + ([tops[span]] if opened else []),
        )
        parts = [jnp.exp(part - top) for part in parts]
        total = functools.reduce(
            jnp.add, [jnp.sum(part, axis=-1, keepdims=True) for part in parts]
        )
        mixed = functools.reduce(
            jnp.add, [mm(part.astype(BF16), key) for part, key in zip(parts, keys)]
        )
        if opened:
            fade = jnp.exp(tops[span] - top)
            total = total + fade * sums[span]
            mixed = mixed + fade * mixes[span]
        return span, top, total, mixed

    def keep(span, top, total, mixed):
        tops[span] = top
        sums[span] = total
        mixes[span] = mixed

    groups = n_t // group
    arrive(twin)
    for i in range(groups):
        keep(*fold(i, [context[n_t], context[0], context[twin]], masked=True, opened=False))
    for p in near_chips:
        for k in cores(p):
            arrive(k)
    if near_chips:
        for i in range(groups):
            keep(*fold(i, [chip(p) for p in near_chips]))

    for k in cores(far):
        arrive(k)
    for i in [*range(groups // 2, groups), *range(1, groups // 2), 0]:
        _, _, total, mixed = fold(i, [chip(far)])
        attended = (mixed * (1.0 / total)).astype(BF16)
        for g in range(group):
            k = i * group + g
            out = mm(attended[g * every : (g + 1) * every], wuv_in[k])
            for h in range(heads):
                own = out[h * tokens : (h + 1) * tokens, h * hd : (h + 1) * hd] * row_alive
                result_out[k, :, h * hd : (h + 1) * hd] = own.astype(BF16)
            if k:
                back_copy(k).start()
    mla_ref[mine] = result_out[0]

    for k in range(1, n_t):
        back_copy(k).wait_recv()
    for k in range(1, n_t):
        lift_copy(k).wait_send()
        wuv_copy(k).wait_send()
        page_copy(k).wait_send()
        back_copy(k).wait_send()
    for which in range(2):
        for k in range(1, side[which]):
            first_leg(which, k).wait_send()
        for j in range(1, side[1 - which]):
            column = incoming.at[pl.ds(spot(which, 1, 0, 0), side[which])]
            pltpu.make_async_copy(column, column, send_sem.at[which, 1, j]).wait()


def run_fused(
    sizes,
    tool_len,
    state_table,
    page_table,
    kda_pool,
    latent_pool,
    kda_q,
    kda_k,
    kda_v,
    kda_gate,
    kda_beta,
    mla_q,
    mla_new,
    w_uk,
    w_uv,
):
    heads, slots, hd, _ = kda_pool.shape
    _, pool_pages, page_len, latent = latent_pool.shape
    rows, tokens, _ = kda_q.shape
    pages_row = pool_pages // rows
    n_z, n_y, n_t = sizes
    n_dp = n_z * n_y
    lanes = state_table.shape[1]
    vmem = pl.BlockSpec(memory_space=pltpu.VMEM)
    smem = pl.BlockSpec(memory_space=pltpu.SMEM)
    out = pltpu.VMEM((2,) + kda_q.shape, BF16)
    dma = pltpu.SemaphoreType.DMA
    both = pl.pallas_call(
        functools.partial(fused, sizes),
        out_shape=out,
        in_specs=[smem] + [pl.BlockSpec(memory_space=pl.ANY)] * 13,
        out_specs=vmem,
        scratch_shapes=[
            pltpu.VMEM((heads * slots + pool_pages, hd, hd), BF16),
            pltpu.VMEM(kda_q.shape, BF16),
            pltpu.VMEM(kda_k.shape, BF16),
            pltpu.VMEM(kda_v.shape, BF16),
            pltpu.VMEM(kda_gate.shape, BF16),
            pltpu.VMEM(kda_beta.shape, BF16),
            pltpu.VMEM(mla_q.shape, BF16),
            pltpu.VMEM(mla_new.shape, BF16),
            pltpu.VMEM(w_uk.shape, BF16),
            pltpu.VMEM((latent, heads * hd), BF16),
            pltpu.VMEM((2 * heads, lanes), jnp.int32),
            pltpu.VMEM(page_table.shape[1:], jnp.int32),
            pltpu.VMEM((2, lanes), jnp.int32),
            pltpu.VMEM((1, LANES), jnp.int32),
            pltpu.SMEM((2, lanes), jnp.int32),
            pltpu.SMEM((1, LANES), jnp.int32),
            pltpu.VMEM((2, n_z, n_y, hd, hd), BF16),
            pltpu.VMEM((4 * n_dp, hd, hd), BF16),
            pltpu.VMEM((rows, heads, tokens, latent), BF16),
            pltpu.VMEM((n_t, heads, tokens, latent), BF16),
            pltpu.VMEM((n_t, latent, heads * hd), BF16),
            pltpu.VMEM((rows, pages_row * page_len, latent), BF16),
            pltpu.VMEM((n_t + 1, pages_row * page_len, latent), BF16),
            pltpu.VMEM((n_t, tokens, heads * hd), BF16),
            pltpu.VMEM((rows, heads * tokens, hd), F32),
            pltpu.VMEM((rows, heads * tokens, hd), F32),
            pltpu.VMEM((n_t * heads * tokens, 1), F32),
            pltpu.VMEM((n_t * heads * tokens, 1), F32),
            pltpu.VMEM((n_t * heads * tokens, latent), F32),
            dma((2, 2, max(n_z, n_y))),
            dma((2, max(n_z, n_y))),
            dma((2, max(n_z, n_y))),
        ]
        + [dma((n_t,))] * 8
        + [dma((heads + latent // hd,)), dma((8 + heads,)), dma((4,))],
        compiler_params=pltpu.CompilerParams(
            collective_id=0, has_side_effects=True, vmem_limit_bytes=60 * 1024 * 1024
        ),
    )(
        tool_len,
        state_table,
        page_table,
        kda_pool,
        latent_pool,
        kda_q,
        kda_k,
        kda_v,
        kda_gate,
        kda_beta,
        mla_q,
        mla_new,
        w_uk,
        w_uv,
    )
    return both[0], both[1]


def local(
    tool_len,
    state_table,
    page_table,
    kda_pool,
    latent_pool,
    kda_q,
    kda_k,
    kda_v,
    kda_gate,
    kda_beta,
    mla_q,
    mla_new,
    w_uk,
    w_uv,
):
    n_dp, n_t = lax.axis_size("dp"), lax.axis_size("tensor")
    return run_fused(
        (n_dp // SIDE_Y, SIDE_Y, n_t),
        tool_len,
        state_table.T,
        jnp.transpose(page_table, (1, 2, 0)),
        kda_pool,
        latent_pool,
        kda_q,
        kda_k,
        kda_v,
        kda_gate,
        jnp.transpose(kda_beta, (0, 2, 1)),
        mla_q,
        mla_new,
        w_uk,
        w_uv,
    )


def solution(mesh):
    in_specs = (
        P("dp"),
        P(),
        P(),
        P("tensor", "dp", None, None),
        P("tensor", "dp", None, None),
        P("dp", None, "tensor"),
        P("dp", None, "tensor"),
        P("dp", None, "tensor"),
        P("dp", None, "tensor"),
        P("dp", None, "tensor"),
        P("dp", None, "tensor"),
        P("dp", None, None),
        P("tensor", None, None),
        P("tensor", None, None),
    )
    out_specs = (P("dp", None, "tensor"), P("dp", None, "tensor"))
    return jax.shard_map(local, mesh=mesh, in_specs=in_specs, out_specs=out_specs, check_vma=False)
```
